256 devices in a mesh: seq: 16 (over x, y), vocab: 16 (over z, core).
Axes of the slice: x: 4, y: 4, z: 8, core: 2. Of those that a mesh axis runs over, the one named last changes fastest.
Arguments:
- hidden: bfloat16 [16, 2048, 4608], P('seq', None, 'vocab'), may hold values from -60 to 60
- picks: int32 [16, 64], P('seq'), may hold values from 0 to 2047
- counts: int32 [16], P('seq'), may hold values from 1 to 64, 512 in all
- norm_gain: float32 [4608], P('vocab'), may hold values from 0.5 to 1.5
- head_weight: bfloat16 [196608, 4608], P(('vocab', 'seq')), may hold values from -3 to 3
Outputs:
- log_probs: float32 [1024, 196608], P('seq', 'vocab')
The draws below stay inside these ranges and needn't reach their ends.
Inputs may be any that keep to these rules, and one draw needn't show every extreme that they name: The counts sum to exactly 512, and the largest is exactly 64.
All inputs are finite; a program needn't handle non-finite values. No bound on the sum of `counts` on one device may be relied on, other than what follows from the above.
Results may differ from the reference program's by a relative error of at most 0.00034.
Values may be sent and summed in bfloat16 or wider, within the bound.
A program may use at most 64 MiB of HBM per device.

```python
import math
import jax
import jax.numpy as jnp
import numpy as np
from jax import lax

D = 4608
CAP = 64
SEQ_LEN = 2048
GROUPS = 16
TOTAL = 512
VOCAB = 196608


def draw_hidden(key, part):
    key = jax.random.fold_in(key, 5)
    base_key, column_key, row_key = jax.random.split(key, 3)
    column_scale = jnp.exp(jnp.linspace(0.0, jnp.log(5.0), D) + jax.random.uniform(column_key, (D,), minval=-0.35, maxval=0.35))
    row_scale = jnp.exp(jax.random.uniform(row_key, (GROUPS, SEQ_LEN, 1), minval=0.0, maxval=jnp.log(10.0)))
    values = jnp.clip(jax.random.normal(base_key, (GROUPS, SEQ_LEN, D)), -4.0, 4.0)
    return (values * row_scale * column_scale[None, None, :] * 0.2).astype(jnp.bfloat16)


def draw_head_weight(key, part):
    key = jax.random.fold_in(key, 9)
    base_key, jitter_key = jax.random.split(key, 2)
    trend = jnp.exp(jnp.linspace(jnp.log(0.5), jnp.log(3.0), VOCAB))
    jitter = jnp.exp(jax.random.uniform(jitter_key, (VOCAB,), minval=-0.35, maxval=0.35))
    row_scale = (trend * jitter)[:, None] / jnp.sqrt(float(D))
    values = jnp.clip(jax.random.normal(base_key, (VOCAB, D)), -4.0, 4.0)
    return (values * row_scale).astype(jnp.bfloat16)


def set_ends(drawn, stream_key, least, largest):
    longest = drawn.shape.index(max(drawn.shape))
    spots = []
    for shift in (0, 1):
        where = [jax.random.randint(jax.random.fold_in(stream_key, axis), (), 0, length) for axis, length in enumerate(drawn.shape)]
        where[longest] = (where[longest] + shift) % drawn.shape[longest]
        spots.append(tuple(where))
    return drawn.at[spots[0]].set(least).at[spots[1]].set(largest)


def length_profile(count, total, most, lean):
    weights = [(1 << 20) // math.isqrt(grade ** lean) + 1 for grade in range(2, count + 1)]
    surplus, holding = total - most - (count - 1), [1] * (count - 1)
    while surplus > 0:
        candidates = [i for i in range(count - 1) if holding[i] < most]
        whole, budget = sum([weights[i] for i in candidates]), surplus
        for i in candidates:
            extra = min(most - holding[i], max(1, budget * weights[i] // whole), surplus)
            holding[i] = holding[i] + extra
            surplus = surplus - extra
    return np.array([most] + holding)


def ragged(own_key, count, total, reach, skew):
    if count == 2:
        one = jax.random.randint(own_key, (), max(1, total - reach), min(reach, total - 1) + 1)
        return jnp.stack([one, total - one])
    tallies = jnp.asarray(length_profile(count, total, reach, skew), jnp.int32)
    pairs = (count - 1) // 2
    giver, taker = tallies[1:1 + 2 * pairs:2], tallies[2:2 + 2 * pairs:2]
    margin = jnp.minimum(giver - 1, reach - taker)
    shifted = jax.random.randint(jax.random.fold_in(own_key, 1), (pairs,), 0, 1 << 20) % (margin + 1)
    tallies = tallies.at[1:1 + 2 * pairs:2].set(giver - shifted).at[2:2 + 2 * pairs:2].set(taker + shifted)
    return tallies[jax.random.permutation(jax.random.fold_in(own_key, 2), count)]


def setup_inputs(seed: int = 0) -> dict:
    streams_of = jax.random.split(jax.random.key(seed), 6)
    return {
        "hidden": draw_hidden(jax.random.fold_in(streams_of[5], 71), 0),
        "picks": set_ends(jax.random.randint(streams_of[1], (GROUPS, CAP), 0, SEQ_LEN), jax.random.fold_in(streams_of[1], 1), 0, SEQ_LEN - 1).astype(jnp.int32),
        "counts": ragged(streams_of[2], GROUPS, TOTAL, CAP, 2).astype(jnp.int32),
        "norm_gain": jnp.clip(1.0 + 0.1 * jax.random.normal(streams_of[3], (D,), jnp.float32), 0.5, 1.5),
        "head_weight": draw_head_weight(jax.random.fold_in(streams_of[5], 71), 0),
    }


SOFT_CAP = 30.0
EPSILON = 1e-06

def soft_capped(values):
    return SOFT_CAP * jnp.tanh(values / SOFT_CAP)

def choose(sequence, chosen):
    return jnp.take(sequence, chosen, axis=0)

def reference(hidden, picks, counts, norm_gain, head_weight):
    group_count = picks.shape[0]
    slot_count = picks.shape[1]
    selected = jax.vmap(choose)(hidden, picks).reshape(group_count * slot_count, hidden.shape[2])
    as_float = selected.astype(jnp.float32)
    mean_square = lax.optimization_barrier(jnp.mean(as_float * as_float, axis=1))
    normed = (as_float * lax.rsqrt(mean_square + EPSILON)[:, None] * norm_gain[None, :]).astype(jnp.bfloat16)

    def group_probs(row_block):
        capped = soft_capped(jnp.dot(row_block, head_weight.T, preferred_element_type=jnp.float32))
        partition = lax.optimization_barrier(jnp.sum(jnp.exp(capped), axis=1))
        return capped - jnp.log(partition)[:, None]
    grouped = lax.map(group_probs, normed.reshape(group_count, slot_count, hidden.shape[2]))
    live_mask = lax.iota(jnp.int32, slot_count)[None, :] < counts[:, None]
    masked = jnp.where(live_mask[:, :, None], grouped, jnp.zeros_like(grouped))
    return masked.reshape(group_count * slot_count, grouped.shape[2])
```

```python
import functools

import jax
import jax.numpy as jnp
from jax import lax
from jax.experimental import pallas as pl
from jax.experimental.pallas import tpu as pltpu
from jax.sharding import PartitionSpec as P

SOFT_CAP = 30.0
EPSILON = 1e-06
CODE = 32767.0
HALF = 16
MESH = pl.DeviceIdType.MESH


def iota(shape, dim):
    return lax.broadcasted_iota(jnp.int32, shape, dim)


def kernel(
    dims,
    hidden_ref,
    picks_ref,
    counts_ref,
    gain_ref,
    head_ref,
    codes_ref,
    logs_ref,
    head,
    cnt,
    sqs,
    place,
    placed,
    feats,
    rows_x,
    level,
    expo,
    send,
    sums_a,
    sums_b,
    head_sem,
    own_sem,
    cnt_s, cnt_r,
    sqs_s, sqs_r,
    plc_s, plc_r,
    fea_s, fea_r,
    sib_s, sib_r,
    one_s, one_r,
    two_s, two_r,
    fwd_s, fwd_r,
    out_s, out_r,
    sma_s, sma_r,
    smb_s, smb_r,
):
    n_seq, n_vocab, side, slots, total = dims
    rows = total // n_seq
    width = head_ref.shape[1]
    entries = head_ref.shape[0]
    features = hidden_ref.shape[0]
    half_width = width // 2
    n_z = n_vocab // 2
    s = lax.axis_index("seq")
    v = lax.axis_index("vocab")
    x, y = s // side, s % side
    z, core = v // 2, v % 2
    sibling = 2 * z + (1 - core)

    def seq_peer(p):
        return (s + p) % n_seq

    def vocab_peer(p):
        return (v + p) % n_vocab

    load_head = pltpu.make_async_copy(head_ref, head, head_sem)
    load_head.start()

    barrier = pltpu.get_barrier_semaphore()

    def greet_seq(p, c):
        pl.semaphore_signal(barrier, inc=1, device_id={"seq": seq_peer(p)}, device_id_type=MESH)
        return c

    def greet_vocab(p, c):
        pl.semaphore_signal(barrier, inc=1, device_id={"vocab": vocab_peer(p)}, device_id_type=MESH)
        return c

    lax.fori_loop(1, n_seq, greet_seq, 0)
    lax.fori_loop(1, n_vocab, greet_vocab, 0)
    pl.semaphore_wait(barrier, n_seq + n_vocab - 2)

    def exchange(count, axis, peer, src, dst, send_sem, recv_sem):
        def copy(p):
            return pltpu.make_async_remote_copy(
                src_ref=src(p), dst_ref=dst, send_sem=send_sem.at[p], recv_sem=recv_sem.at[p],
                device_id={axis: peer(p)}, device_id_type=MESH,
            )

        def begin(p, c):
            copy(p).start()
            return c

        def wait_recv(p, c):
            copy(p).wait_recv()
            return c

        def wait_send(p, c):
            copy(p).wait_send()
            return c

        def start():
            lax.fori_loop(1, count, begin, 0)

        def received():
            lax.fori_loop(1, count, wait_recv, 0)

        def sent():
            lax.fori_loop(1, count, wait_send, 0)

        return start, received, sent

    cnt[pl.ds(s, 1)] = jnp.full((1, 8, 128), counts_ref[0], jnp.int32)
    cnt_start, cnt_received, cnt_sent = exchange(
        n_seq, "seq", seq_peer, lambda p: cnt.at[s], cnt.at[s], cnt_s, cnt_r
    )
    cnt_start()

    one_hot = (iota((hidden_ref.shape[1], slots), 0) == picks_ref[...]).astype(jnp.bfloat16)
    selected = jnp.dot(hidden_ref[...], one_hot, preferred_element_type=jnp.float32)
    square = jnp.sum(selected * selected, axis=0, keepdims=True)
    square = jnp.concatenate([square, jnp.zeros((1, 128 - slots), jnp.float32)], axis=1)
    sqs[pl.ds(v, 1)] = jnp.broadcast_to(square, (8, 128))[None]
    sqs_start, sqs_received, sqs_sent = exchange(
        n_vocab, "vocab", vocab_peer, lambda p: sqs.at[v], sqs.at[v], sqs_s, sqs_r
    )
    sqs_start()
    diagonal = iota((features, features), 0) == iota((features, features), 1)
    gain = jnp.sum(jnp.where(diagonal, gain_ref[...], 0.0), axis=1, keepdims=True)

    cnt_received()
    group = iota((n_seq, 8, 128), 0)
    every = cnt[...]
    offset = jnp.sum(jnp.where(group < s, every, 0), axis=0)[0:1, 0:1]
    count = jnp.sum(jnp.where(group == s, every, 0), axis=0)[0:1, 0:1]

    slot = iota((total, slots), 1)
    placing = ((iota((total, slots), 0) == offset + slot) & (slot < count)).astype(jnp.bfloat16)

    sqs_received()
    mean_square = jnp.sum(sqs[...], axis=0)[0:1, 0:slots] / width
    normed = (selected * lax.rsqrt(mean_square + EPSILON) * gain).astype(jnp.bfloat16)

    compact = lax.dot_general(
        placing, normed, (((1,), (1,)), ((), ())), preferred_element_type=jnp.float32
    ).astype(jnp.bfloat16)
    place[...] = compact.reshape(n_seq, rows, features)
    plc_start, plc_received, plc_sent = exchange(
        n_seq, "seq", seq_peer, lambda p: place.at[seq_peer(p)], placed.at[s], plc_s, plc_r
    )
    plc_start()
    placed[pl.ds(s, 1)] = place[pl.ds(s, 1)]
    plc_received()
    block = jnp.sum(placed[...].astype(jnp.float32), axis=0).astype(jnp.bfloat16)

    feats[pl.ds(v, 1)] = block[None]

    def z_peer(p):
        return 2 * ((z + p) % n_z) + core

    fea_start, fea_received, fea_sent = exchange(
        n_z, "vocab", z_peer, lambda p: feats.at[v], feats.at[v], fea_s, fea_r
    )
    fea_start()

    def hand_over(p):
        of = 2 * ((z + n_z - p) % n_z) + core
        return pltpu.make_async_remote_copy(
            src_ref=feats.at[of], dst_ref=feats.at[of], send_sem=sib_s.at[p], recv_sem=sib_r.at[p],
            device_id={"vocab": sibling}, device_id_type=MESH,
        )

    hand_over(0).start()

    def pass_on(p, c):
        pltpu.make_async_remote_copy(
            src_ref=feats.at[v], dst_ref=feats.at[v], send_sem=fea_s.at[p], recv_sem=fea_r.at[p],
            device_id={"vocab": z_peer(p)}, device_id_type=MESH,
        ).wait_recv()
        hand_over(p).start()
        return c

    def handed(p, c):
        hand_over(p).wait_recv()
        return c

    def handed_off(p, c):
        hand_over(p).wait_send()
        return c

    lax.fori_loop(1, n_z, pass_on, 0)
    lax.fori_loop(0, n_z, handed, 0)
    own = jnp.concatenate([feats[i] for i in range(n_vocab)], axis=1)
    for k in range(2):
        part = own[:, k * half_width : (k + 1) * half_width]
        rows_x[0, k, 0, pl.ds(x, 1)] = part[:HALF][None]
        rows_x[0, k, 1, pl.ds(y, 1)] = part[HALF:][None]

    def across(order, p):
        if order == 0:
            return ((x + p) % side) * side + y
        return x * side + (y + p) % side

    def spot(order, j):
        return ((x if order == 0 else y) + side - j) % side

    def first(order, p):
        at = rows_x.at[0, core, order, spot(order, 0)]
        return pltpu.make_async_remote_copy(
            src_ref=at, dst_ref=at, send_sem=one_s.at[order, p], recv_sem=one_r.at[order, p],
            device_id={"seq": across(order, p)}, device_id_type=MESH,
        )

    def second(order, p, j):
        return pltpu.make_async_remote_copy(
            src_ref=rows_x.at[0, core, order, spot(order, j)],
            dst_ref=rows_x.at[p, core, order, spot(order, j)],
            send_sem=two_s.at[order, p, j], recv_sem=two_r.at[order, p, j],
            device_id={"seq": across(1 - order, p)}, device_id_type=MESH,
        )

    def over(kind, order, p, j):
        at = rows_x.at[p, kind, order, spot(order, j)]
        return pltpu.make_async_remote_copy(
            src_ref=at, dst_ref=at, send_sem=fwd_s.at[order, p, j], recv_sem=fwd_r.at[order, p, j],
            device_id={"vocab": sibling}, device_id_type=MESH,
        )

    near = [p for d in range(1, side // 2 + 1) for p in sorted({d, side - d})]
    for p in near:
        for order in range(2):
            first(order, p).start()
    for p in near:
        for order in range(2):
            second(order, p, 0).start()
    for j in near:
        for order in range(2):
            first(order, j).wait_recv()
            for p in near:
                second(order, p, j).start()
            over(core, order, 0, j).start()

    load_head.wait()
    level[pl.ds(total, slots)] = jnp.zeros((slots, entries), jnp.int32)
    columns = 256 if entries % 256 == 0 else entries

    def multiply(p):
        def some(i, total_exp):
            at = pl.ds(pl.multiple_of(i * columns, columns), columns)
            logits = jnp.zeros((2 * side * HALF, columns), jnp.float32)
            for k in range(2):
                logits += lax.dot_general(
                    rows_x[p, k].reshape(2 * side * HALF, half_width),
                    head[at, k * half_width : (k + 1) * half_width],
                    (((1,), (1,)), ((), ())),
                    preferred_element_type=jnp.float32,
                )
            bent = jnp.tanh(logits / SOFT_CAP)
            code = jnp.round(bent * CODE).astype(jnp.int32)
            for order in range(2):
                for piece in range(side):
                    low = (order * side + piece) * HALF
                    level[pl.ds(pl.multiple_of(row_of(p, order, piece), HALF), HALF), at] = code[low : low + HALF]
            e = jnp.exp(SOFT_CAP * bent)
            for c in range(0, columns, 128):
                total_exp += e[:, c : c + 128]
            return total_exp

        total_exp = lax.fori_loop(
            0, entries // columns, some, jnp.zeros((2 * side * HALF, 128), jnp.float32)
        )
        summed = jnp.broadcast_to(jnp.sum(total_exp, axis=1, keepdims=True), total_exp.shape)
        for order in range(2):
            for piece in range(side):
                low = (order * side + piece) * HALF
                expo[pl.ds(pl.multiple_of(row_of(p, order, piece), HALF), HALF)] = summed[low : low + HALF]

    def row_of(p, order, piece):
        if order == 0:
            return (piece * side + (y + side - p) % side) * rows
        return (((x + side - p) % side) * side + piece) * rows + HALF

    for j in near:
        for order in range(2):
            over(1 - core, order, 0, j).wait_recv()
    multiply(0)
    for p in near:
        for j in [0] + near:
            for order in range(2):
                second(order, p, j).wait_recv()
                over(core, order, p, j).start()
        for j in [0] + near:
            for order in range(2):
                over(1 - core, order, p, j).wait_recv()
        multiply(p)

    square_eye = iota((128, 128), 0) == iota((128, 128), 1)
    lines = [
        jnp.sum(jnp.where(square_eye, expo[i * 128 : (i + 1) * 128], 0.0), axis=0, keepdims=True)
        for i in range(total // 128)
    ]
    lines.append(jnp.zeros((8 - len(lines), 128), jnp.float32))
    sums_a[pl.ds(s, 1)] = jnp.concatenate(lines, axis=0)[None]
    sma_start, sma_received, sma_sent = exchange(
        n_seq, "seq", seq_peer, lambda p: sums_a.at[s], sums_a.at[s], sma_s, sma_r
    )
    sma_start()


    def result(p):
        return pltpu.make_async_remote_copy(
            src_ref=send.at[p], dst_ref=codes_ref.at[s], send_sem=out_s.at[p], recv_sem=out_r.at[p],
            device_id={"seq": seq_peer(p)}, device_id_type=MESH,
        )

    def fill(p):
        start = jnp.sum(jnp.where(group < seq_peer(p), cnt[...], 0), axis=0)[0:1, 0:1]
        for c in range(0, entries, 128):
            window = level[:, c : c + 128]
            bit = 1 << (total.bit_length() - 2)
            while bit:
                left = bit - 1 + slots if bit > 8 else slots + 8
                left = (left + 7) // 8 * 8
                if bit >= 8:
                    window = jnp.where(start & bit != 0, window[bit : bit + left], window[:left])
                else:
                    window = jnp.where(start & bit != 0, pltpu.roll(window, left - bit, axis=0), window)
                bit //= 2
            send[pl.ds(p, 1), :, c : c + 128] = window[:slots].astype(jnp.int16)[None]

    def give(p, c):
        fill(p)
        result(p).start()
        return c

    lax.fori_loop(1, n_seq, give, 0)
    fill(0)
    keep = pltpu.make_async_copy(send.at[0], codes_ref.at[s], own_sem)
    keep.start()

    sma_received()
    sums_b[pl.ds(v, 1)] = jnp.sum(sums_a[...], axis=0)[None]
    smb_start, smb_received, smb_sent = exchange(
        n_vocab, "vocab", vocab_peer, lambda p: sums_b.at[v], sums_b.at[v], smb_s, smb_r
    )
    smb_start()
    smb_received()
    partition = jnp.sum(sums_b[...], axis=0)
    mine = jnp.zeros((slots, 1), jnp.float32)
    for i in range(total // 128):
        hit = iota((slots, 128), 1) + 128 * i == offset + iota((slots, 128), 0)
        mine += jnp.sum(jnp.where(hit, partition[i : i + 1], 0.0), axis=1, keepdims=True)
    logs_ref[...] = jnp.broadcast_to(jnp.log(jnp.where(mine > 0.0, mine, 1.0)), logs_ref.shape)

    cnt_sent()
    sqs_sent()
    plc_sent()
    fea_sent()
    lax.fori_loop(0, n_z, handed_off, 0)
    for order in range(2):
        for p in near:
            first(order, p).wait_send()
        for j in near:
            over(core, order, 0, j).wait_send()
        for p in near:
            for j in [0] + near:
                second(order, p, j).wait_send()
                over(core, order, p, j).wait_send()
    sma_sent()
    smb_sent()
    keep.wait()

    def got(p, c):
        result(p).wait()
        return c

    lax.fori_loop(1, n_seq, got, 0)


def solution(mesh):
    n_seq, n_vocab = mesh.shape["seq"], mesh.shape["vocab"]
    side = int(round(n_seq**0.5))

    def local(hidden, picks, counts, norm_gain, head_weight):
        slots = picks.shape[1]
        entries, width = head_weight.shape
        features = hidden.shape[2]
        total = n_seq * slots // 2
        rows = total // n_seq
        dma = lambda *shape: [pltpu.SemaphoreType.DMA(shape)] * 2
        vmem = pl.BlockSpec(memory_space=pltpu.VMEM)
        hbm = pl.BlockSpec(memory_space=pl.ANY)
        codes, logs = pl.pallas_call(
            functools.partial(kernel, (n_seq, n_vocab, side, slots, total)),
            out_shape=(
                jax.ShapeDtypeStruct((n_seq, slots, entries), jnp.int16),
                jax.ShapeDtypeStruct((slots, 128), jnp.float32),
            ),
            in_specs=[vmem, vmem, pl.BlockSpec(memory_space=pltpu.SMEM), vmem, hbm],
            out_specs=(hbm, vmem),
            scratch_shapes=[
                pltpu.VMEM((entries, width), jnp.bfloat16),
                pltpu.VMEM((n_seq, 8, 128), jnp.int32),
                pltpu.VMEM((n_vocab, 8, 128), jnp.float32),
                pltpu.VMEM((n_seq, rows, features), jnp.bfloat16),
                pltpu.VMEM((n_seq, rows, features), jnp.bfloat16),
                pltpu.VMEM((n_vocab, rows, features), jnp.bfloat16),
                pltpu.VMEM((side, 2, 2, side, HALF, width // 2), jnp.bfloat16),
                pltpu.VMEM((total + slots, entries), jnp.int32),
                pltpu.VMEM((total, 128), jnp.float32),
                pltpu.VMEM((n_seq, slots, entries), jnp.int16),
                pltpu.VMEM((n_seq, 8, 128), jnp.float32),
                pltpu.VMEM((n_vocab, 8, 128), jnp.float32),
                pltpu.SemaphoreType.DMA,
                pltpu.SemaphoreType.DMA,
                *dma(n_seq),
                *dma(n_vocab),
                *dma(n_seq),
                *dma(n_vocab // 2),
                *dma(n_vocab // 2),
                *dma(2, side),
                *dma(2, side, side),
                *dma(2, side, side),
                *dma(n_seq),
                *dma(n_seq),
                *dma(n_vocab),
            ],
            compiler_params=pltpu.CompilerParams(
                collective_id=0, has_side_effects=True, vmem_limit_bytes=48 << 20
            ),
            cost_estimate=pl.CostEstimate(
                flops=2 * total * entries * width, bytes_accessed=2 * entries * width, transcendentals=2 * total * entries
            ),
        )(jnp.swapaxes(hidden[0], 0, 1), picks, counts, norm_gain[None], head_weight)
        capped = codes.astype(jnp.float32) * (SOFT_CAP / CODE)
        log_rows = jnp.swapaxes(capped, 0, 1).reshape(slots, n_seq * entries) - logs[:, :1]
        live = lax.iota(jnp.int32, slots) < counts[0]
        return jnp.where(live[:, None], log_rows, 0.0)

    in_specs = (
        P("seq", None, "vocab"),
        P("seq", None),
        P("seq"),
        P("vocab"),
        P(("vocab", "seq"), None),
    )
    return jax.shard_map(local, mesh=mesh, in_specs=in_specs, out_specs=P("seq", "vocab"), check_vma=False)
```

```python
import functools

import jax
import jax.numpy as jnp
from jax import lax
from jax.experimental import pallas as pl
from jax.experimental.pallas import tpu as pltpu
from jax.sharding import PartitionSpec as P

SOFT_CAP = 30.0
EPSILON = 1e-06
CODE = 32767.0
HALF = 16
MESH = pl.DeviceIdType.MESH


def iota(shape, dim):
    return lax.broadcasted_iota(jnp.int32, shape, dim)


def kernel(
    dims,
    hidden_ref,
    picks_ref,
    counts_ref,
    gain_ref,
    head_ref,
    codes_ref,
    logs_ref,
    hidden,
    picks,
    gain,
    head,
    cnt,
    gains,
    place,
    placed,
    feats,
    rows_x,
    partial,
    level,
    expo,
    send,
    sums_a,
    sums_b,
    in_sem,
    own_sem,
    cnt_sem,
    gain_sem,
    plc_sem,
    sma_sem,
    smb_sem,
    out_sem,
    fea_s, fea_r,
    sib_s, sib_r,
    one_s, one_r,
    two_s, two_r,
    fwd_s, fwd_r,
):
    n_seq, n_vocab, side, slots, total = dims
    rows = total // n_seq
    width = head_ref.shape[1]
    entries = head_ref.shape[0]
    features = hidden_ref.shape[0]
    block_rows = 2 * side * HALF
    half_width = width // 2
    n_z = n_vocab // 2
    s = lax.axis_index("seq")
    v = lax.axis_index("vocab")
    x, y = s // side, s % side
    z, core = v // 2, v % 2
    sibling = 2 * z + (1 - core)

    def seq_peer(p):
        return (s + p) % n_seq

    def vocab_peer(p):
        return (v + p) % n_vocab

    loads = [
        pltpu.make_async_copy(ref, to, in_sem.at[i])
        for i, (ref, to) in enumerate(
            [(hidden_ref, hidden), (picks_ref, picks), (gain_ref, gain), (head_ref, head)]
        )
    ]
    for load in loads:
        load.start()

    barrier = pltpu.get_barrier_semaphore()

    def greet_seq(p, c):
        pl.semaphore_signal(barrier, inc=1, device_id={"seq": seq_peer(p)}, device_id_type=MESH)
        return c

    def greet_vocab(p, c):
        pl.semaphore_signal(barrier, inc=1, device_id={"vocab": vocab_peer(p)}, device_id_type=MESH)
        return c

    lax.fori_loop(1, n_seq, greet_seq, 0)
    lax.fori_loop(1, n_vocab, greet_vocab, 0)
    pl.semaphore_wait(barrier, n_seq + n_vocab - 2)

    def exchange(count, axis, peer, src, dst, many, sems, prepare=None):
        def copy(p, src, dst):
            return pltpu.make_async_remote_copy(
                src_ref=src, dst_ref=dst, send_sem=sems.at[0], recv_sem=sems.at[1],
                device_id={axis: peer(p)}, device_id_type=MESH,
            )

        def begin(p, c):
            if prepare is not None:
                prepare(p)
            copy(p, src(p), dst).start()
            return c

        def start():
            lax.fori_loop(1, count, begin, 0)

        def received():
            copy(1, many, many).wait_recv()

        def sent():
            copy(1, many, many).wait_send()

        return start, received, sent

    cnt[pl.ds(s, 1)] = jnp.full((1, 8, 128), counts_ref[0], jnp.int32)
    cnt_start, cnt_received, cnt_sent = exchange(
        n_seq, "seq", seq_peer, lambda p: cnt.at[s], cnt.at[s], cnt.at[pl.ds(0, n_seq - 1)], cnt_sem
    )
    cnt_start()

    loads[0].wait()
    loads[1].wait()
    one_hot = (iota((hidden.shape[1], slots), 0) == picks[...]).astype(jnp.bfloat16)
    selected = jnp.dot(hidden[...], one_hot, preferred_element_type=jnp.float32).astype(jnp.bfloat16)

    loads[2].wait()
    gains[pl.ds(v, 1)] = jnp.broadcast_to(gain[...].reshape(1, 1, features), (1, 8, features))
    gain_start, gain_received, gain_sent = exchange(
        n_vocab, "vocab", vocab_peer, lambda p: gains.at[v], gains.at[v], gains.at[pl.ds(0, n_vocab - 1)], gain_sem
    )
    gain_start()

    cnt_received()
    group = iota((n_seq, 8, 128), 0)
    every = cnt[...]
    offset = jnp.sum(jnp.where(group < s, every, 0), axis=0)[0:1, 0:1]
    count = jnp.sum(jnp.where(group == s, every, 0), axis=0)[0:1, 0:1]

    slot = iota((total, slots), 1)
    placing = ((iota((total, slots), 0) == offset + slot) & (slot < count)).astype(jnp.bfloat16)

    compact = lax.dot_general(
        placing, selected, (((1,), (1,)), ((), ())), preferred_element_type=jnp.float32
    ).astype(jnp.bfloat16)
    place[...] = compact.reshape(n_seq, rows, features)
    plc_start, plc_received, plc_sent = exchange(
        n_seq, "seq", seq_peer, lambda p: place.at[seq_peer(p)], placed.at[s], placed.at[pl.ds(0, n_seq - 1)], plc_sem
    )
    plc_start()
    placed[pl.ds(s, 1)] = place[pl.ds(s, 1)]
    plc_received()
    block = jnp.sum(placed[...].astype(jnp.float32), axis=0).astype(jnp.bfloat16)

    feats[pl.ds(v, 1)] = block[None]

    def z_peer(p):
        return 2 * ((z + p) % n_z) + core

    def along(p):
        return pltpu.make_async_remote_copy(
            src_ref=feats.at[v], dst_ref=feats.at[v], send_sem=fea_s.at[p], recv_sem=fea_r.at[p],
            device_id={"vocab": z_peer(p)}, device_id_type=MESH,
        )

    def set_out(p, c):
        along(p).start()
        return c

    def set_off(p, c):
        along(p).wait_send()
        return c

    lax.fori_loop(1, n_z, set_out, 0)

    def hand_over(p):
        of = 2 * ((z + n_z - p) % n_z) + core
        return pltpu.make_async_remote_copy(
            src_ref=feats.at[of], dst_ref=feats.at[of], send_sem=sib_s.at[p], recv_sem=sib_r.at[p],
            device_id={"vocab": sibling}, device_id_type=MESH,
        )

    hand_over(0).start()

    def pass_on(p, c):
        along(p).wait_recv()
        hand_over(p).start()
        return c

    def handed(p, c):
        hand_over(p).wait_recv()
        return c

    def handed_off(p, c):
        hand_over(p).wait_send()
        return c

    lax.fori_loop(1, n_z, pass_on, 0)
    lax.fori_loop(0, n_z, handed, 0)
    gain_received()
    raw = jnp.concatenate([feats[i] for i in range(n_vocab)], axis=1).astype(jnp.float32)
    scale = jnp.concatenate([gains[i, 0:1] for i in range(n_vocab)], axis=1)
    mean_square = jnp.sum(raw * raw, axis=1, keepdims=True) / width
    own = (raw * lax.rsqrt(mean_square + EPSILON) * scale).astype(jnp.bfloat16)
    for k in range(2):
        part = own[:, k * half_width : (k + 1) * half_width]
        rows_x[0, k, 0, 0] = part[:HALF]
        rows_x[0, k, 1, 0] = part[HALF:]

    def across(order, p):
        if order == 0:
            return ((x + p) % side) * side + y
        return x * side + (y + p) % side

    def first(order, j):
        return pltpu.make_async_remote_copy(
            src_ref=rows_x.at[0, core, order, 0], dst_ref=rows_x.at[j, core, order, 0],
            send_sem=one_s.at[order, j], recv_sem=one_r.at[order, j],
            device_id={"seq": across(order, j)}, device_id_type=MESH,
        )

    def second(order, j, p):
        return pltpu.make_async_remote_copy(
            src_ref=rows_x.at[j, core, order, 0], dst_ref=rows_x.at[j, core, order, p],
            send_sem=two_s.at[order, j, p], recv_sem=two_r.at[order, j, p],
            device_id={"seq": across(1 - order, p)}, device_id_type=MESH,
        )

    def over(kind, order, j, p):
        at = rows_x.at[j, kind, order, p]
        return pltpu.make_async_remote_copy(
            src_ref=at, dst_ref=at, send_sem=fwd_s.at[order, j, p], recv_sem=fwd_r.at[order, j, p],
            device_id={"vocab": sibling}, device_id_type=MESH,
        )

    near = [p for d in range(1, side // 2 + 1) for p in sorted({d, side - d})]
    for j in near:
        for order in range(2):
            first(order, j).start()
    for p in near:
        for order in range(2):
            second(order, 0, p).start()
    for j in near:
        for order in range(2):
            first(order, j).wait_recv()
            for p in near:
                second(order, j, p).start()
            over(core, order, j, 0).start()

    loads[3].wait()
    level[pl.ds(total, slots)] = jnp.zeros((slots, entries), jnp.int32)
    columns = 256 if entries % 256 == 0 else entries

    def row_of(order, j, p):
        if order == 0:
            return ((x + side - j) % side * side + (y + side - p) % side) * rows
        return ((x + side - p) % side * side + (y + side - j) % side) * rows + HALF

    def product(j, k, i):
        at = pl.ds(pl.multiple_of(i * columns, columns), columns)
        return at, lax.dot_general(
            rows_x[j, k].reshape(block_rows, half_width),
            head[at, pl.ds(pl.multiple_of(k * half_width, half_width), half_width)],
            (((1,), (1,)), ((), ())),
            preferred_element_type=jnp.float32,
        )

    def begin_block(j):
        def some(i, c):
            at, logits = product(j, core, i)
            partial[:, at] = logits
            return c

        lax.fori_loop(0, entries // columns, some, 0)

    def end_block(j):
        def some(i, total_exp):
            at, logits = product(j, 1 - core, i)
            bent = jnp.tanh((logits + partial[:, at]) / SOFT_CAP)
            code = jnp.round(bent * CODE).astype(jnp.int32)
            for order in range(2):
                for p in range(side):
                    low = (order * side + p) * HALF
                    level[pl.ds(pl.multiple_of(row_of(order, j, p), HALF), HALF), at] = code[low : low + HALF]
            e = jnp.exp(SOFT_CAP * bent)
            for c in range(0, columns, 128):
                total_exp += e[:, c : c + 128]
            return total_exp

        total_exp = lax.fori_loop(0, entries // columns, some, jnp.zeros((block_rows, 128), jnp.float32))
        summed = jnp.broadcast_to(jnp.sum(total_exp, axis=1, keepdims=True), total_exp.shape)
        for order in range(2):
            for p in range(side):
                low = (order * side + p) * HALF
                expo[pl.ds(pl.multiple_of(row_of(order, j, p), HALF), HALF)] = summed[low : low + HALF]

    for j in [0] + near:
        for p in near:
            for order in range(2):
                second(order, j, p).wait_recv()
                over(core, order, j, p).start()
        begin_block(j)
        for p in near + ([0] if j else []):
            for order in range(2):
                over(1 - core, order, j, p).wait_recv()
        end_block(j)

    square_eye = iota((128, 128), 0) == iota((128, 128), 1)
    lines = [
        jnp.sum(jnp.where(square_eye, expo[i * 128 : (i + 1) * 128], 0.0), axis=0, keepdims=True)
        for i in range(total // 128)
    ]
    lines.append(jnp.zeros((8 - len(lines), 128), jnp.float32))
    sums_a[pl.ds(s, 1)] = jnp.concatenate(lines, axis=0)[None]
    sma_start, sma_received, sma_sent = exchange(
        n_seq, "seq", seq_peer, lambda p: sums_a.at[s], sums_a.at[s], sums_a.at[pl.ds(0, n_seq - 1)], sma_sem
    )
    sma_start()


    def fill(p):
        start = jnp.sum(jnp.where(group < seq_peer(p), cnt[...], 0), axis=0)[0:1, 0:1]
        for c in range(0, entries, 128):
            window = level[:, c : c + 128]
            bit = 1 << (total.bit_length() - 2)
            while bit:
                left = bit - 1 + slots if bit > 8 else slots + 8
                left = (left + 7) // 8 * 8
                if bit >= 8:
                    window = jnp.where(start & bit != 0, window[bit : bit + left], window[:left])
                else:
                    window = jnp.where(start & bit != 0, pltpu.roll(window, left - bit, axis=0), window)
                bit //= 2
            send[pl.ds(p, 1), :, c : c + 128] = window[:slots].astype(jnp.int16)[None]

    out_start, out_received, out_sent = exchange(
        n_seq, "seq", seq_peer, lambda p: send.at[p], codes_ref.at[s], codes_ref.at[pl.ds(0, n_seq - 1)], out_sem, fill
    )

    out_start()
    fill(0)
    keep = pltpu.make_async_copy(send.at[0], codes_ref.at[s], own_sem)
    keep.start()

    sma_received()
    sums_b[pl.ds(v, 1)] = jnp.sum(sums_a[...], axis=0)[None]
    smb_start, smb_received, smb_sent = exchange(
        n_vocab, "vocab", vocab_peer, lambda p: sums_b.at[v], sums_b.at[v], sums_b.at[pl.ds(0, n_vocab - 1)], smb_sem
    )
    smb_start()
    smb_received()
    partition = jnp.sum(sums_b[...], axis=0)
    mine = jnp.zeros((slots, 1), jnp.float32)
    for i in range(total // 128):
        hit = iota((slots, 128), 1) + 128 * i == offset + iota((slots, 128), 0)
        mine += jnp.sum(jnp.where(hit, partition[i : i + 1], 0.0), axis=1, keepdims=True)
    logs_ref[...] = jnp.broadcast_to(jnp.log(jnp.where(mine > 0.0, mine, 1.0)), logs_ref.shape)

    cnt_sent()
    gain_sent()
    plc_sent()
    lax.fori_loop(1, n_z, set_off, 0)
    lax.fori_loop(0, n_z, handed_off, 0)
    for order in range(2):
        for j in near:
            first(order, j).wait_send()
            over(core, order, j, 0).wait_send()
        for j in [0] + near:
            for p in near:
                second(order, j, p).wait_send()
                over(core, order, j, p).wait_send()
    sma_sent()
    smb_sent()
    keep.wait()
    out_received()
    out_sent()


def decode(counts_ref, codes_ref, logs_ref, out_ref):
    blocks, slots, entries = codes_ref.shape
    live = iota((slots, entries), 0) < counts_ref[0]
    for i in range(blocks):
        capped = codes_ref[i].astype(jnp.float32) * (SOFT_CAP / CODE)
        out_ref[:, i * entries : (i + 1) * entries] = jnp.where(live, capped - logs_ref[:, :1], 0.0)


def solution(mesh):
    n_seq, n_vocab = mesh.shape["seq"], mesh.shape["vocab"]
    side = int(round(n_seq**0.5))

    def local(hidden, picks, counts, norm_gain, head_weight):
        slots = picks.shape[1]
        entries, width = head_weight.shape
        positions, features = hidden.shape[1:]
        total = n_seq * slots // 2
        rows = total // n_seq
        dma = lambda *shape: [pltpu.SemaphoreType.DMA(shape)] * 2
        vmem = pl.BlockSpec(memory_space=pltpu.VMEM)
        hbm = pl.BlockSpec(memory_space=pl.ANY)
        codes, logs = pl.pallas_call(
            functools.partial(kernel, (n_seq, n_vocab, side, slots, total)),
            out_shape=(
                jax.ShapeDtypeStruct((n_seq, slots, entries), jnp.int16),
                jax.ShapeDtypeStruct((slots, 128), jnp.float32),
            ),
            in_specs=[hbm, hbm, pl.BlockSpec(memory_space=pltpu.SMEM), hbm, hbm],
            out_specs=(hbm, vmem),
            scratch_shapes=[
                pltpu.VMEM((features, positions), jnp.bfloat16),
                pltpu.VMEM((1, slots), jnp.int32),
                pltpu.VMEM((features,), jnp.float32),
                pltpu.VMEM((entries, width), jnp.bfloat16),
                pltpu.VMEM((n_seq, 8, 128), jnp.int32),
                pltpu.VMEM((n_vocab, 8, features), jnp.float32),
                pltpu.VMEM((n_seq, rows, features), jnp.bfloat16),
                pltpu.VMEM((n_seq, rows, features), jnp.bfloat16),
                pltpu.VMEM((n_vocab, rows, features), jnp.bfloat16),
                pltpu.VMEM((side, 2, 2, side, HALF, width // 2), jnp.bfloat16),
                pltpu.VMEM((2 * side * HALF, entries), jnp.float32),
                pltpu.VMEM((total + slots, entries), jnp.int32),
                pltpu.VMEM((total, 128), jnp.float32),
                pltpu.VMEM((n_seq, slots, entries), jnp.int16),
                pltpu.VMEM((n_seq, 8, 128), jnp.float32),
                pltpu.VMEM((n_vocab, 8, 128), jnp.float32),
                pltpu.SemaphoreType.DMA((4,)),
                pltpu.SemaphoreType.DMA,
                *[pltpu.SemaphoreType.DMA((2,))] * 6,
                *dma(n_vocab // 2),
                *dma(n_vocab // 2),
                *dma(2, side),
                *dma(2, side, side),
                *dma(2, side, side),
            ],
            compiler_params=pltpu.CompilerParams(
                collective_id=0, has_side_effects=True, vmem_limit_bytes=48 << 20
            ),
            cost_estimate=pl.CostEstimate(
                flops=2 * total * entries * width, bytes_accessed=2 * entries * width, transcendentals=2 * total * entries
            ),
        )(jnp.swapaxes(hidden[0], 0, 1), picks, counts, norm_gain, head_weight)
        step = max(1, n_seq // 4)
        return pl.pallas_call(
            decode,
            grid=(n_seq // step,),
            out_shape=jax.ShapeDtypeStruct((slots, n_seq * entries), jnp.float32),
            in_specs=[
                pl.BlockSpec(memory_space=pltpu.SMEM),
                pl.BlockSpec((step, slots, entries), lambda i: (i, 0, 0)),
                pl.BlockSpec((slots, 128), lambda i: (0, 0)),
            ],
            out_specs=pl.BlockSpec((slots, step * entries), lambda i: (0, i)),
        )(counts, codes, logs)

    in_specs = (
        P("seq", None, "vocab"),
        P("seq", None),
        P("seq"),
        P("vocab"),
        P(("vocab", "seq"), None),
    )
    return jax.shard_map(local, mesh=mesh, in_specs=in_specs, out_specs=P("seq", "vocab"), check_vma=False)
```

```python
import functools

import jax
import jax.numpy as jnp
from jax import lax
from jax.experimental import pallas as pl
from jax.experimental.pallas import tpu as pltpu
from jax.sharding import PartitionSpec as P

SOFT_CAP = 30.0
EPSILON = 1e-06
CODE = 32767.0
HALF = 16
COLUMNS = 256
VMEM_BYTES = 63 << 20
MESH = pl.DeviceIdType.MESH


def iota(shape, dim):
    return lax.broadcasted_iota(jnp.int32, shape, dim)


def kernel(
    dims,
    hidden_ref,
    picks_ref,
    counts_ref,
    gain_ref,
    head_ref,
    codes_ref,
    terms_ref,
    hidden,
    picks,
    gain,
    head,
    cnt,
    gains,
    squares,
    place,
    placed,
    block_out,
    feats,
    rows_x,
    partial,
    level,
    expo,
    send,
    terms,
    sums_a,
    sums_b,
    in_sem,
    terms_sem,
    own_sem,
    cnt_sem,
    gain_sem,
    sqs_sem,
    plc_sem,
    fea_sem,
    sma_sem,
    smb_sem,
    out_s, out_r,
    one_s, one_r,
    two_s, two_r,
    fwd_s, fwd_r,
):
    n_seq, n_vocab, side, slots, total = dims
    rows = total // n_seq
    width = head_ref.shape[1]
    entries = head_ref.shape[0]
    features = hidden_ref.shape[0]
    block_rows = 2 * side * HALF
    half_width = width // 2
    n_z = n_vocab // 2
    s = lax.axis_index("seq")
    v = lax.axis_index("vocab")
    x, y = s // side, s % side
    z, core = v // 2, v % 2
    sibling = 2 * z + (1 - core)

    def seq_peer(p):
        return (s + p) % n_seq

    def vocab_peer(p):
        return (v + p) % n_vocab

    loads = [
        pltpu.make_async_copy(ref, to, in_sem.at[i])
        for i, (ref, to) in enumerate(
            [(hidden_ref, hidden), (picks_ref, picks), (gain_ref, gain), (head_ref, head)]
        )
    ]
    for load in loads:
        load.start()

    barrier = pltpu.get_barrier_semaphore()

    def greet_seq(p, c):
        pl.semaphore_signal(barrier, inc=1, device_id={"seq": seq_peer(p)}, device_id_type=MESH)
        return c

    def greet_vocab(p, c):
        pl.semaphore_signal(barrier, inc=1, device_id={"vocab": vocab_peer(p)}, device_id_type=MESH)
        return c

    lax.fori_loop(1, n_seq, greet_seq, 0)
    lax.fori_loop(1, n_vocab, greet_vocab, 0)
    pl.semaphore_wait(barrier, n_seq + n_vocab - 2)

    def hops(p, size):
        return min(p, size - p)

    seq_steps = sorted(
        ((a, b) for a in range(side) for b in range(side) if a or b),
        key=lambda step: hops(step[0], side) + hops(step[1], side),
    )

    def exchange(axis, peers, src, dst, many, sems):
        def copy(peer, src, dst):
            return pltpu.make_async_remote_copy(
                src_ref=src, dst_ref=dst, send_sem=sems.at[0], recv_sem=sems.at[1],
                device_id={axis: peer}, device_id_type=MESH,
            )

        def start():
            for peer in peers:
                copy(peer, src(peer), dst).start()

        def received():
            copy(peers[0], many, many).wait_recv()

        def sent():
            copy(peers[0], many, many).wait_send()

        return start, received, sent

    seq_peers = [(x + a) % side * side + (y + b) % side for a, b in seq_steps]
    vocab_peers = [vocab_peer(p) for p in sorted(range(1, n_vocab), key=lambda p: -hops(p, n_vocab))]

    cnt[pl.ds(s, 1)] = jnp.full((1, 8, 128), counts_ref[0], jnp.int32)
    cnt_start, cnt_received, cnt_sent = exchange(
        "seq", seq_peers, lambda peer: cnt.at[s], cnt.at[s], cnt.at[pl.ds(0, n_seq - 1)], cnt_sem
    )
    cnt_start()

    loads[0].wait()
    loads[1].wait()
    one_hot = (iota((hidden.shape[1], slots), 0) == picks[...]).astype(jnp.bfloat16)
    selected = jnp.dot(hidden[...], one_hot, preferred_element_type=jnp.float32).astype(jnp.bfloat16)

    loads[2].wait()
    line = gain[...].reshape(1, features)
    line = jnp.concatenate([line, jnp.zeros((1, -features % 128), jnp.float32)], axis=1)
    lines = [line[:, c : c + 128] for c in range(0, line.shape[1], 128)]
    lines.append(jnp.zeros((8 - len(lines), 128), jnp.float32))
    gains[pl.ds(v, 1)] = jnp.concatenate(lines, axis=0)[None]
    gain_start, gain_received, gain_sent = exchange(
        "vocab", vocab_peers, lambda peer: gains.at[v], gains.at[v], gains.at[pl.ds(0, n_vocab - 1)], gain_sem
    )
    gain_start()

    cnt_received()
    group = iota((n_seq, 8, 128), 0)
    every = cnt[...]
    offset = jnp.sum(jnp.where(group < s, every, 0), axis=0)[0:1, 0:1]
    count = jnp.sum(jnp.where(group == s, every, 0), axis=0)[0:1, 0:1]

    slot = iota((total, slots), 1)
    placing = ((iota((total, slots), 0) == offset + slot) & (slot < count)).astype(jnp.bfloat16)

    compact = lax.dot_general(
        placing, selected, (((1,), (1,)), ((), ())), preferred_element_type=jnp.float32
    ).astype(jnp.bfloat16)
    place[...] = compact.reshape(n_seq, rows, features)
    plc_start, plc_received, plc_sent = exchange(
        "seq", seq_peers, lambda peer: place.at[peer], placed.at[s], placed.at[pl.ds(0, n_seq - 1)], plc_sem
    )
    plc_start()
    placed[pl.ds(s, 1)] = place[pl.ds(s, 1)]
    plc_received()
    block = jnp.sum(placed[...].astype(jnp.float32), axis=0).astype(jnp.bfloat16)

    wide = block.astype(jnp.float32)
    row_eye = iota((rows, 128), 0) == iota((rows, 128), 1)
    square = jnp.sum(jnp.where(row_eye, jnp.sum(wide * wide, axis=1, keepdims=True), 0.0), axis=0, keepdims=True)
    squares[pl.ds(v, 1)] = jnp.broadcast_to(square, (8, 128))[None]
    sqs_start, sqs_received, sqs_sent = exchange(
        "vocab", vocab_peers, lambda peer: squares.at[v], squares.at[v], squares.at[pl.ds(0, n_vocab - 1)], sqs_sem
    )

    part_of = z // (n_z // 2)
    kept = core == part_of
    mine = v - part_of * n_z

    def along(p, src, dst):
        return pltpu.make_async_remote_copy(
            src_ref=src, dst_ref=dst, send_sem=fea_sem.at[0], recv_sem=fea_sem.at[1],
            device_id={"vocab": 2 * ((z + p) % n_z) + part_of}, device_id_type=MESH,
        )

    block_out[...] = block
    for p in sorted(range(1, n_z), key=lambda p: -hops(p, n_z)):
        along(p, block_out, feats.at[mine]).start()

    @pl.when(kept)
    def _():
        feats[pl.ds(mine, 1)] = block[None]

    @pl.when(jnp.logical_not(kept))
    def _():
        along(0, block_out, feats.at[mine]).start()

    sqs_start()

    @pl.when(kept)
    def _():
        many = feats.at[pl.ds(0, n_z - 1)]
        along(1, many, many).wait_recv()

    @pl.when(jnp.logical_not(kept))
    def _():
        along(1, feats, feats).wait_recv()

    gain_received()
    sqs_received()
    raw = jnp.concatenate([feats[i] for i in range(n_z)], axis=1).astype(jnp.float32)
    held = gains[pl.ds(core * n_z, n_z)]
    scale = jnp.concatenate(
        [held[i, c // 128 : c // 128 + 1, : min(128, features - c)] for i in range(n_z) for c in range(0, features, 128)],
        axis=1,
    )
    mean_square = jnp.sum(squares[...], axis=0)[0:1] / width
    mean_square = jnp.sum(jnp.where(row_eye, mean_square, 0.0), axis=1, keepdims=True)
    own = (raw * lax.rsqrt(mean_square + EPSILON) * scale).astype(jnp.bfloat16)
    rows_x[0, pl.ds(core, 1), 0, 0] = own[:HALF][None]
    rows_x[0, pl.ds(core, 1), 1, 0] = own[HALF:][None]

    def across(order, p):
        if order == 0:
            return ((x + p) % side) * side + y
        return x * side + (y + p) % side

    def first(order, j):
        return pltpu.make_async_remote_copy(
            src_ref=rows_x.at[0, core, order, 0], dst_ref=rows_x.at[j, core, order, 0],
            send_sem=one_s.at[order, j], recv_sem=one_r.at[order, j],
            device_id={"seq": across(order, j)}, device_id_type=MESH,
        )

    def second(order, j, p):
        return pltpu.make_async_remote_copy(
            src_ref=rows_x.at[j, core, order, 0], dst_ref=rows_x.at[j, core, order, p],
            send_sem=two_s.at[order, j, p], recv_sem=two_r.at[order, j, p],
            device_id={"seq": across(1 - order, p)}, device_id_type=MESH,
        )

    def over(kind, order, j, p):
        at = rows_x.at[j, kind, order, p]
        return pltpu.make_async_remote_copy(
            src_ref=at, dst_ref=at, send_sem=fwd_s.at[order, j, p], recv_sem=fwd_r.at[order, j, p],
            device_id={"vocab": sibling}, device_id_type=MESH,
        )

    near = [p for d in range(1, side // 2 + 1) for p in sorted({d, side - d})]
    for j in near:
        for order in range(2):
            first(order, j).start()
    for p in near:
        for order in range(2):
            second(order, 0, p).start()
    for order in range(2):
        over(core, order, 0, 0).start()
    for j in near:
        for order in range(2):
            first(order, j).wait_recv()
            for p in near:
                second(order, j, p).start()
            over(core, order, j, 0).start()

    loads[3].wait()
    level[pl.ds(total, slots)] = jnp.zeros((slots, entries), jnp.int32)
    rounds = entries // COLUMNS

    def row_of(order, j, p):
        if order == 0:
            return ((x + side - j) % side * side + (y + side - p) % side) * rows
        return ((x + side - p) % side * side + (y + side - j) % side) * rows + HALF

    def product(j, k, i):
        at = pl.ds(pl.multiple_of(i * COLUMNS, COLUMNS), COLUMNS)
        return at, lax.dot_general(
            rows_x[j, k].reshape(block_rows, half_width),
            head[at, pl.ds(pl.multiple_of(k * half_width, half_width), half_width)],
            (((1,), (1,)), ((), ())),
            preferred_element_type=jnp.float32,
        )

    def fill(i):
        at = i * COLUMNS

        def one(g, c):
            start = jnp.sum(jnp.where(group < g, cnt[...], 0), axis=0)[0:1, 0:1]
            for low in range(0, COLUMNS, 128):
                window = level[:, pl.ds(pl.multiple_of(at + low, 128), 128)]
                bit = 1 << (total.bit_length() - 2)
                while bit:
                    left = bit - 1 + slots if bit > 8 else slots + 8
                    left = (left + 7) // 8 * 8
                    if bit >= 8:
                        window = jnp.where(start & bit != 0, window[bit : bit + left], window[:left])
                    else:
                        window = jnp.where(start & bit != 0, pltpu.roll(window, left - bit, axis=0), window)
                    bit //= 2
                send[pl.ds(i, 1), pl.ds(g, 1), :, low : low + 128] = window[:slots].astype(jnp.int16)[None, None]
            return c

        lax.fori_loop(0, n_seq, one, 0)
        keep(i).start()

    def keep(i):
        return pltpu.make_async_copy(send.at[i, s], codes_ref.at[i, s], own_sem.at[i])

    def returned(i, peer, src, dst):
        return pltpu.make_async_remote_copy(
            src_ref=src, dst_ref=dst, send_sem=out_s.at[i], recv_sem=out_r.at[i],
            device_id={"seq": peer}, device_id_type=MESH,
        )

    def give(i):
        for peer in seq_peers:
            returned(i, peer, send.at[i, peer], codes_ref.at[i, s]).start()

    def all_returned(i):
        many = codes_ref.at[i, pl.ds(0, n_seq - 1)]
        return returned(i, seq_peers[0], many, many)

    last = near[-1]

    def begin_block(j):
        def some(i, c):
            at, logits = product(j, core, i)
            partial[:, at] = logits
            return c

        lax.fori_loop(0, rounds, some, 0)

    def end_block(j):
        def some(i, total_exp):
            at, logits = product(j, 1 - core, i)
            bent = jnp.tanh((logits + partial[:, at]) / SOFT_CAP)
            code = jnp.round(bent * CODE).astype(jnp.int32)
            for order in range(2):
                for p in range(side):
                    low = (order * side + p) * HALF
                    level[pl.ds(pl.multiple_of(row_of(order, j, p), HALF), HALF), at] = code[low : low + HALF]
            e = jnp.exp(SOFT_CAP * bent)
            for c in range(0, COLUMNS, 128):
                total_exp += e[:, c : c + 128]
            if j == last:
                fill(i)

                @pl.when(i == 0)
                def _():
                    give(0)

            return total_exp

        total_exp = lax.fori_loop(0, rounds, some, jnp.zeros((block_rows, 128), jnp.float32))
        summed = jnp.broadcast_to(jnp.sum(total_exp, axis=1, keepdims=True), total_exp.shape)
        for order in range(2):
            for p in range(side):
                low = (order * side + p) * HALF
                expo[pl.ds(pl.multiple_of(row_of(order, j, p), HALF), HALF)] = summed[low : low + HALF]

    for j in [0] + near:
        for p in near:
            for order in range(2):
                second(order, j, p).wait_recv()
                over(core, order, j, p).start()
        begin_block(j)
        for p in [0] + near:
            for order in range(2):
                over(1 - core, order, j, p).wait_recv()
        end_block(j)

    square_eye = iota((128, 128), 0) == iota((128, 128), 1)
    lines = [
        jnp.sum(jnp.where(square_eye, expo[i * 128 : (i + 1) * 128], 0.0), axis=0, keepdims=True)
        for i in range(total // 128)
    ]
    lines.append(jnp.zeros((8 - len(lines), 128), jnp.float32))
    sums_a[pl.ds(s, 1)] = jnp.concatenate(lines, axis=0)[None]
    sma_start, sma_received, sma_sent = exchange(
        "seq", seq_peers, lambda peer: sums_a.at[s], sums_a.at[s], sums_a.at[pl.ds(0, n_seq - 1)], sma_sem
    )
    sma_start()

    for i in range(1, rounds):
        give(i)

    sma_received()
    sums_b[pl.ds(v, 1)] = jnp.sum(sums_a[...], axis=0)[None]
    smb_start, smb_received, smb_sent = exchange(
        "vocab", vocab_peers, lambda peer: sums_b.at[v], sums_b.at[v], sums_b.at[pl.ds(0, n_vocab - 1)], smb_sem
    )
    smb_start()
    smb_received()
    partition = jnp.sum(sums_b[...], axis=0)
    total_of = jnp.zeros((slots, 1), jnp.float32)
    for i in range(total // 128):
        hit = iota((slots, 128), 1) + 128 * i == offset + iota((slots, 128), 0)
        total_of += jnp.sum(jnp.where(hit, partition[i : i + 1], 0.0), axis=1, keepdims=True)
    live = iota((slots, 128), 0) < count
    terms[0] = jnp.where(live, SOFT_CAP / CODE, 0.0)
    terms[1] = jnp.where(live, jnp.log(jnp.where(total_of > 0.0, total_of, 1.0)), 0.0)
    write_terms = pltpu.make_async_copy(terms, terms_ref, terms_sem)
    write_terms.start()

    cnt_sent()
    gain_sent()
    plc_sent()
    sqs_sent()

    @pl.when(kept)
    def _():
        many = feats.at[pl.ds(0, n_z - 1)]
        along(1, many, many).wait_send()

    @pl.when(jnp.logical_not(kept))
    def _():
        along(1, feats, feats).wait_send()

    for order in range(2):
        over(core, order, 0, 0).wait_send()
        for j in near:
            first(order, j).wait_send()
            over(core, order, j, 0).wait_send()
        for j in [0] + near:
            for p in near:
                second(order, j, p).wait_send()
                over(core, order, j, p).wait_send()
    sma_sent()
    smb_sent()
    write_terms.wait()
    for i in range(rounds):
        keep(i).wait()
        all_returned(i).wait()


def decode(codes_ref, terms_ref, out_ref, codes, terms, result, codes_sem, terms_sem, out_sem):
    rounds, n_seq, slots, _ = codes_ref.shape
    entries = rounds * COLUMNS
    steps = 4
    step = n_seq // steps
    take_terms = pltpu.make_async_copy(terms_ref, terms, terms_sem)
    take_terms.start()

    def take(k):
        at = pl.ds(k * step, step)
        return pltpu.make_async_copy(codes_ref.at[:, at], codes.at[:, at], codes_sem.at[k])

    def put(k):
        at = pl.ds(k * step * entries, step * entries)
        return pltpu.make_async_copy(result.at[:, at], out_ref.at[:, at], out_sem.at[k])

    for k in range(steps):
        take(k).start()
    take_terms.wait()
    for k in range(steps):
        take(k).wait()
        for g in range(k * step, (k + 1) * step):
            for i in range(rounds):
                for low in range(0, COLUMNS, 128):
                    at = g * entries + i * COLUMNS + low
                    code = codes[i, g, :, low : low + 128].astype(jnp.int32).astype(jnp.float32)
                    result[:, at : at + 128] = code * terms[0] - terms[1]
        put(k).start()
    for k in range(steps):
        put(k).wait()


def solution(mesh):
    n_seq, n_vocab = mesh.shape["seq"], mesh.shape["vocab"]
    side = int(round(n_seq**0.5))

    def local(hidden, picks, counts, norm_gain, head_weight):
        slots = picks.shape[1]
        entries, width = head_weight.shape
        positions, features = hidden.shape[1:]
        total = n_seq * slots // 2
        rows = total // n_seq
        dma = lambda *shape: [pltpu.SemaphoreType.DMA(shape)] * 2
        hbm = pl.BlockSpec(memory_space=pltpu.HBM)
        codes, terms = pl.pallas_call(
            functools.partial(kernel, (n_seq, n_vocab, side, slots, total)),
            out_shape=(
                jax.ShapeDtypeStruct((entries // COLUMNS, n_seq, slots, COLUMNS), jnp.int16),
                jax.ShapeDtypeStruct((2, slots, 128), jnp.float32),
            ),
            in_specs=[hbm, hbm, pl.BlockSpec(memory_space=pltpu.SMEM), hbm, hbm],
            out_specs=(hbm, hbm),
            scratch_shapes=[
                pltpu.VMEM((features, positions), jnp.bfloat16),
                pltpu.VMEM((1, slots), jnp.int32),
                pltpu.VMEM((features,), jnp.float32),
                pltpu.VMEM((entries, width), jnp.bfloat16),
                pltpu.VMEM((n_seq, 8, 128), jnp.int32),
                pltpu.VMEM((n_vocab, 8, 128), jnp.float32),
                pltpu.VMEM((n_vocab, 8, 128), jnp.float32),
                pltpu.VMEM((n_seq, rows, features), jnp.bfloat16),
                pltpu.VMEM((n_seq, rows, features), jnp.bfloat16),
                pltpu.VMEM((rows, features), jnp.bfloat16),
                pltpu.VMEM((n_vocab // 2, rows, features), jnp.bfloat16),
                pltpu.VMEM((side, 2, 2, side, HALF, width // 2), jnp.bfloat16),
                pltpu.VMEM((2 * side * HALF, entries), jnp.float32),
                pltpu.VMEM((total + slots, entries), jnp.int32),
                pltpu.VMEM((total, 128), jnp.float32),
                pltpu.VMEM((entries // COLUMNS, n_seq, slots, COLUMNS), jnp.int16),
                pltpu.VMEM((2, slots, 128), jnp.float32),
                pltpu.VMEM((n_seq, 8, 128), jnp.float32),
                pltpu.VMEM((n_vocab, 8, 128), jnp.float32),
                pltpu.SemaphoreType.DMA((4,)),
                pltpu.SemaphoreType.DMA,
                pltpu.SemaphoreType.DMA((entries // COLUMNS,)),
                *[pltpu.SemaphoreType.DMA((2,))] * 7,
                *dma(entries // COLUMNS),
                *dma(2, side),
                *dma(2, side, side),
                *dma(2, side, side),
            ],
            compiler_params=pltpu.CompilerParams(
                collective_id=0, has_side_effects=True, vmem_limit_bytes=VMEM_BYTES
            ),
            cost_estimate=pl.CostEstimate(
                flops=2 * total * entries * width, bytes_accessed=2 * entries * width, transcendentals=2 * total * entries
            ),
        )(jnp.swapaxes(hidden[0], 0, 1), picks, counts, norm_gain, head_weight)
        return pl.pallas_call(
            decode,
            out_shape=jax.ShapeDtypeStruct((slots, n_seq * entries), jnp.float32),
            in_specs=[hbm, hbm],
            out_specs=hbm,
            scratch_shapes=[
                pltpu.VMEM(codes.shape, codes.dtype),
                pltpu.VMEM(terms.shape, terms.dtype),
                pltpu.VMEM((slots, n_seq * entries), jnp.float32),
                pltpu.SemaphoreType.DMA((4,)),
                pltpu.SemaphoreType.DMA,
                pltpu.SemaphoreType.DMA((4,)),
            ],
            compiler_params=pltpu.CompilerParams(vmem_limit_bytes=VMEM_BYTES),
        )(codes, terms)
    in_specs = (
        P("seq", None, "vocab"),
        P("seq", None),
        P("seq"),
        P("vocab"),
        P(("vocab", "seq"), None),
    )
    return jax.shard_map(local, mesh=mesh, in_specs=in_specs, out_specs=P("seq", "vocab"), check_vma=False)
```

```python
import functools

import jax
import jax.numpy as jnp
from jax import lax
from jax.experimental import pallas as pl
from jax.experimental.pallas import tpu as pltpu
from jax.sharding import PartitionSpec as P

SOFT_CAP = 30.0
EPSILON = 1e-06
CODE = 32767.0
HALF = 16
COLUMNS = 256
VMEM_BYTES = 63 << 20
MESH = pl.DeviceIdType.MESH


def iota(shape, dim):
    return lax.broadcasted_iota(jnp.int32, shape, dim)


def kernel(
    dims,
    hidden_ref,
    picks_ref,
    counts_ref,
    gain_ref,
    head_ref,
    codes_ref,
    terms_ref,
    hidden,
    picks,
    gain,
    head,
    turned,
    cnt,
    gains,
    squares,
    place,
    placed,
    block_out,
    feats,
    rows_x,
    partial,
    level,
    expo,
    send,
    terms,
    sums_a,
    sums_b,
    in_sem,
    terms_sem,
    own_sem,
    cnt_sem,
    gain_sem,
    sqs_sem,
    plc_sem,
    fea_sem,
    sma_sem,
    smb_sem,
    out_s, out_r,
    one_s, one_r,
    two_s, two_r,
    fwd_s, fwd_r,
):
    n_seq, n_vocab, side, slots, total = dims
    rows = total // n_seq
    width = head_ref.shape[1]
    entries = head_ref.shape[0]
    features = hidden_ref.shape[0]
    block_rows = 2 * side * HALF
    half_width = width // 2
    n_z = n_vocab // 2
    s = lax.axis_index("seq")
    v = lax.axis_index("vocab")
    x, y = s // side, s % side
    z, core = v // 2, v % 2
    sibling = 2 * z + (1 - core)

    def seq_peer(p):
        return (s + p) % n_seq

    def vocab_peer(p):
        return (v + p) % n_vocab

    loads = [
        pltpu.make_async_copy(ref, to, in_sem.at[i])
        for i, (ref, to) in enumerate(
            [(hidden_ref, hidden), (picks_ref, picks), (gain_ref, gain), (head_ref, head)]
        )
    ]
    for load in loads:
        load.start()

    barrier = pltpu.get_barrier_semaphore()

    def greet_seq(p, c):
        pl.semaphore_signal(barrier, inc=1, device_id={"seq": seq_peer(p)}, device_id_type=MESH)
        return c

    def greet_vocab(p, c):
        pl.semaphore_signal(barrier, inc=1, device_id={"vocab": vocab_peer(p)}, device_id_type=MESH)
        return c

    lax.fori_loop(1, n_seq, greet_seq, 0)
    lax.fori_loop(1, n_vocab, greet_vocab, 0)
    pl.semaphore_wait(barrier, n_seq + n_vocab - 2)

    def hops(p, size):
        return min(p, size - p)

    seq_steps = sorted(
        ((a, b) for a in range(side) for b in range(side) if a or b),
        key=lambda step: hops(step[0], side) + hops(step[1], side),
    )

    def exchange(axis, peers, src, dst, many, sems):
        def copy(peer, src, dst):
            return pltpu.make_async_remote_copy(
                src_ref=src, dst_ref=dst, send_sem=sems.at[0], recv_sem=sems.at[1],
                device_id={axis: peer}, device_id_type=MESH,
            )

        def start():
            for peer in peers:
                copy(peer, src(peer), dst).start()

        def received():
            copy(peers[0], many, many).wait_recv()

        def sent():
            copy(peers[0], many, many).wait_send()

        return start, received, sent

    seq_peers = [(x + a) % side * side + (y + b) % side for a, b in seq_steps]
    vocab_peers = [vocab_peer(p) for p in sorted(range(1, n_vocab), key=lambda p: -hops(p, n_vocab))]

    cnt[pl.ds(s, 1)] = jnp.full((1, 8, 128), counts_ref[0], jnp.int32)
    cnt_start, cnt_received, cnt_sent = exchange(
        "seq", seq_peers, lambda peer: cnt.at[s], cnt.at[s], cnt.at[pl.ds(0, n_seq - 1)], cnt_sem
    )
    cnt_start()

    loads[0].wait()
    loads[1].wait()
    one_hot = (iota((hidden.shape[1], slots), 0) == picks[...]).astype(jnp.bfloat16)
    selected = jnp.dot(hidden[...], one_hot, preferred_element_type=jnp.float32).astype(jnp.bfloat16)

    turn = 256 if width % 256 == 0 else width // 3

    def turn_some(i, c):
        at = pl.ds(pl.multiple_of(i * turn, turn), turn)
        turned[at, :] = head[:, at].T
        return c

    loads[3].wait()
    thirds = [width // turn * i // 3 for i in range(4)]
    lax.fori_loop(thirds[0], thirds[1], turn_some, 0)

    cnt_received()
    group = iota((n_seq, 8, 128), 0)
    every = cnt[...]
    offset = jnp.sum(jnp.where(group < s, every, 0), axis=0)[0:1, 0:1]
    count = jnp.sum(jnp.where(group == s, every, 0), axis=0)[0:1, 0:1]

    slot = iota((total, slots), 1)
    placing = ((iota((total, slots), 0) == offset + slot) & (slot < count)).astype(jnp.bfloat16)

    compact = lax.dot_general(
        placing, selected, (((1,), (1,)), ((), ())), preferred_element_type=jnp.float32
    ).astype(jnp.bfloat16)
    place[...] = compact.reshape(n_seq, rows, features)
    plc_start, plc_received, plc_sent = exchange(
        "seq", seq_peers, lambda peer: place.at[peer], placed.at[s], placed.at[pl.ds(0, n_seq - 1)], plc_sem
    )
    plc_start()
    loads[2].wait()
    line = gain[...].reshape(1, features)
    line = jnp.concatenate([line, jnp.zeros((1, -features % 128), jnp.float32)], axis=1)
    lines = [line[:, c : c + 128] for c in range(0, line.shape[1], 128)]
    lines.append(jnp.zeros((8 - len(lines), 128), jnp.float32))
    gains[pl.ds(v, 1)] = jnp.concatenate(lines, axis=0)[None]
    gain_start, gain_received, gain_sent = exchange(
        "vocab", vocab_peers, lambda peer: gains.at[v], gains.at[v], gains.at[pl.ds(0, n_vocab - 1)], gain_sem
    )
    gain_start()

    lax.fori_loop(thirds[1], thirds[2], turn_some, 0)
    placed[pl.ds(s, 1)] = place[pl.ds(s, 1)]
    plc_received()
    block = jnp.sum(placed[...].astype(jnp.float32), axis=0).astype(jnp.bfloat16)

    part_of = z // (n_z // 2)
    kept = core == part_of
    mine = v - part_of * n_z

    def along(p, src, dst):
        return pltpu.make_async_remote_copy(
            src_ref=src, dst_ref=dst, send_sem=fea_sem.at[0], recv_sem=fea_sem.at[1],
            device_id={"vocab": 2 * ((z + p) % n_z) + part_of}, device_id_type=MESH,
        )

    block_out[...] = block
    for p in sorted(range(1, n_z), key=lambda p: -hops(p, n_z)):
        along(p, block_out, feats.at[mine]).start()

    @pl.when(kept)
    def _():
        feats[pl.ds(mine, 1)] = block[None]

    @pl.when(jnp.logical_not(kept))
    def _():
        along(0, block_out, feats.at[mine]).start()

    lax.fori_loop(thirds[2], thirds[3], turn_some, 0)

    @pl.when(kept)
    def _():
        many = feats.at[pl.ds(0, n_z - 1)]
        along(1, many, many).wait_recv()

    @pl.when(jnp.logical_not(kept))
    def _():
        along(1, feats, feats).wait_recv()

    raw = jnp.concatenate([feats[i] for i in range(n_z)], axis=1).astype(jnp.float32)

    row_eye = iota((rows, 128), 0) == iota((rows, 128), 1)
    square = jnp.sum(jnp.where(row_eye, jnp.sum(raw * raw, axis=1, keepdims=True), 0.0), axis=0, keepdims=True)
    squares[pl.ds(core, 1)] = jnp.broadcast_to(square, (8, 128))[None]
    tell_squares = pltpu.make_async_remote_copy(
        src_ref=squares.at[core], dst_ref=squares.at[core], send_sem=sqs_sem.at[0], recv_sem=sqs_sem.at[1],
        device_id={"vocab": sibling}, device_id_type=MESH,
    )
    tell_squares.start()
    gain_received()
    held = gains[pl.ds(core * n_z, n_z)]
    scale = jnp.concatenate(
        [held[i, c // 128 : c // 128 + 1, : min(128, features - c)] for i in range(n_z) for c in range(0, features, 128)],
        axis=1,
    )
    tell_squares.wait_recv()
    mean_square = jnp.sum(squares[...], axis=0)[0:1] / width
    mean_square = jnp.sum(jnp.where(row_eye, mean_square, 0.0), axis=1, keepdims=True)
    own = (raw * lax.rsqrt(mean_square + EPSILON) * scale).astype(jnp.bfloat16)
    rows_x[0, pl.ds(core, 1), 0, 0] = own[:HALF][None]
    rows_x[0, pl.ds(core, 1), 1, 0] = own[HALF:][None]

    def across(order, p):
        if order == 0:
            return ((x + p) % side) * side + y
        return x * side + (y + p) % side

    def first(order, j):
        return pltpu.make_async_remote_copy(
            src_ref=rows_x.at[0, core, order, 0], dst_ref=rows_x.at[j, core, order, 0],
            send_sem=one_s.at[order, j], recv_sem=one_r.at[order, j],
            device_id={"seq": across(order, j)}, device_id_type=MESH,
        )

    def second(order, j, p):
        return pltpu.make_async_remote_copy(
            src_ref=rows_x.at[j, core, order, 0], dst_ref=rows_x.at[j, core, order, p],
            send_sem=two_s.at[order, j, p], recv_sem=two_r.at[order, j, p],
            device_id={"seq": across(1 - order, p)}, device_id_type=MESH,
        )

    def over(kind, order, j, p):
        at = rows_x.at[j, kind, order, p]
        return pltpu.make_async_remote_copy(
            src_ref=at, dst_ref=at, send_sem=fwd_s.at[order, j, p], recv_sem=fwd_r.at[order, j, p],
            device_id={"vocab": sibling}, device_id_type=MESH,
        )

    near = [p for d in range(1, side // 2 + 1) for p in sorted({d, side - d})]
    for j in near:
        for order in range(2):
            first(order, j).start()
    for p in near:
        for order in range(2):
            second(order, 0, p).start()
    for order in range(2):
        over(core, order, 0, 0).start()
    for j in near:
        for order in range(2):
            first(order, j).wait_recv()
            for p in near:
                second(order, j, p).start()
            over(core, order, j, 0).start()

    level[pl.ds(total, slots)] = jnp.zeros((slots, entries), jnp.int32)
    rounds = entries // COLUMNS

    def row_of(order, j, p):
        if order == 0:
            return ((x + side - j) % side * side + (y + side - p) % side) * rows
        return ((x + side - p) % side * side + (y + side - j) % side) * rows + HALF

    def product(j, k, i):
        at = pl.ds(pl.multiple_of(i * COLUMNS, COLUMNS), COLUMNS)
        return at, lax.dot_general(
            rows_x[j, k].reshape(block_rows, half_width),
            turned[pl.ds(pl.multiple_of(k * half_width, half_width), half_width), at],
            (((1,), (0,)), ((), ())),
            preferred_element_type=jnp.float32,
        )

    def fill(i):
        at = i * COLUMNS

        def one(g, c):
            start = jnp.sum(jnp.where(group < g, cnt[...], 0), axis=0)[0:1, 0:1]
            for low in range(0, COLUMNS, 128):
                window = level[:, pl.ds(pl.multiple_of(at + low, 128), 128)]
                bit = 1 << (total.bit_length() - 2)
                while bit:
                    left = bit - 1 + slots if bit > 8 else slots + 8
                    left = (left + 7) // 8 * 8
                    if bit >= 8:
                        window = jnp.where(start & bit != 0, window[bit : bit + left], window[:left])
                    else:
                        window = jnp.where(start & bit != 0, pltpu.roll(window, left - bit, axis=0), window)
                    bit //= 2
                send[pl.ds(i, 1), pl.ds(g, 1), :, low : low + 128] = window[:slots].astype(jnp.int16)[None, None]
            return c

        lax.fori_loop(0, n_seq, one, 0)
        keep(i).start()

    def keep(i):
        return pltpu.make_async_copy(send.at[i, s], codes_ref.at[i, s], own_sem.at[i])

    def returned(i, peer, src, dst):
        return pltpu.make_async_remote_copy(
            src_ref=src, dst_ref=dst, send_sem=out_s.at[i], recv_sem=out_r.at[i],
            device_id={"seq": peer}, device_id_type=MESH,
        )

    def give(i):
        for peer in seq_peers:
            returned(i, peer, send.at[i, peer], codes_ref.at[i, s]).start()

    def all_returned(i):
        many = codes_ref.at[i, pl.ds(0, n_seq - 1)]
        return returned(i, seq_peers[0], many, many)

    last = near[-1]

    def begin_block(j):
        def some(i, c):
            at, logits = product(j, core, i)
            partial[:, at] = logits
            return c

        lax.fori_loop(0, rounds, some, 0)

    def end_block(j):
        def some(i, total_exp):
            at, logits = product(j, 1 - core, i)
            bent = jnp.tanh((logits + partial[:, at]) / SOFT_CAP)
            code = jnp.round(bent * CODE).astype(jnp.int32)
            for order in range(2):
                for p in range(side):
                    low = (order * side + p) * HALF
                    level[pl.ds(pl.multiple_of(row_of(order, j, p), HALF), HALF), at] = code[low : low + HALF]
            e = jnp.exp(SOFT_CAP * bent)
            for c in range(0, COLUMNS, 128):
                total_exp += e[:, c : c + 128]
            if j == last:
                fill(i)

                @pl.when(i == 0)
                def _():
                    give(0)

            return total_exp

        total_exp = lax.fori_loop(0, rounds, some, jnp.zeros((block_rows, 128), jnp.float32))
        summed = jnp.broadcast_to(jnp.sum(total_exp, axis=1, keepdims=True), total_exp.shape)
        for order in range(2):
            for p in range(side):
                low = (order * side + p) * HALF
                expo[pl.ds(pl.multiple_of(row_of(order, j, p), HALF), HALF)] = summed[low : low + HALF]

    for j in [0] + near:
        for p in near:
            for order in range(2):
                second(order, j, p).wait_recv()
                over(core, order, j, p).start()
        begin_block(j)
        for p in [0] + near:
            for order in range(2):
                over(1 - core, order, j, p).wait_recv()
        end_block(j)

    square_eye = iota((128, 128), 0) == iota((128, 128), 1)
    lines = [
        jnp.sum(jnp.where(square_eye, expo[i * 128 : (i + 1) * 128], 0.0), axis=0, keepdims=True)
        for i in range(total // 128)
    ]
    lines.append(jnp.zeros((8 - len(lines), 128), jnp.float32))
    sums_a[pl.ds(s, 1)] = jnp.concatenate(lines, axis=0)[None]
    sma_start, sma_received, sma_sent = exchange(
        "seq", seq_peers, lambda peer: sums_a.at[s], sums_a.at[s], sums_a.at[pl.ds(0, n_seq - 1)], sma_sem
    )
    sma_start()

    for i in range(1, rounds):
        give(i)

    sma_received()
    sums_b[pl.ds(v, 1)] = jnp.sum(sums_a[...], axis=0)[None]
    smb_start, smb_received, smb_sent = exchange(
        "vocab", vocab_peers, lambda peer: sums_b.at[v], sums_b.at[v], sums_b.at[pl.ds(0, n_vocab - 1)], smb_sem
    )
    smb_start()
    smb_received()
    partition = jnp.sum(sums_b[...], axis=0)
    total_of = jnp.zeros((slots, 1), jnp.float32)
    for i in range(total // 128):
        hit = iota((slots, 128), 1) + 128 * i == offset + iota((slots, 128), 0)
        total_of += jnp.sum(jnp.where(hit, partition[i : i + 1], 0.0), axis=1, keepdims=True)
    live = iota((slots, 128), 0) < count
    terms[0] = jnp.where(live, SOFT_CAP / CODE, 0.0)
    terms[1] = jnp.where(live, jnp.log(jnp.where(total_of > 0.0, total_of, 1.0)), 0.0)
    write_terms = pltpu.make_async_copy(terms, terms_ref, terms_sem)
    write_terms.start()

    cnt_sent()
    gain_sent()
    plc_sent()
    tell_squares.wait_send()

    @pl.when(kept)
    def _():
        many = feats.at[pl.ds(0, n_z - 1)]
        along(1, many, many).wait_send()

    @pl.when(jnp.logical_not(kept))
    def _():
        along(1, feats, feats).wait_send()

    for order in range(2):
        over(core, order, 0, 0).wait_send()
        for j in near:
            first(order, j).wait_send()
            over(core, order, j, 0).wait_send()
        for j in [0] + near:
            for p in near:
                second(order, j, p).wait_send()
                over(core, order, j, p).wait_send()
    sma_sent()
    smb_sent()
    write_terms.wait()
    for i in range(rounds):
        keep(i).wait()
        all_returned(i).wait()


def decode(codes_ref, terms_ref, out_ref, codes, terms, result, codes_sem, terms_sem, out_sem):
    rounds, n_seq, slots, _ = codes_ref.shape
    entries = rounds * COLUMNS
    steps = 4
    step = n_seq // steps
    take_terms = pltpu.make_async_copy(terms_ref, terms, terms_sem)
    take_terms.start()

    def take(k):
        at = pl.ds(k * step, step)
        return pltpu.make_async_copy(codes_ref.at[:, at], codes.at[:, at], codes_sem.at[k])

    def put(k):
        at = pl.ds(k * step * entries, step * entries)
        return pltpu.make_async_copy(result.at[:, at], out_ref.at[:, at], out_sem.at[k])

    for k in range(steps):
        take(k).start()
    take_terms.wait()
    for k in range(steps):
        take(k).wait()
        for g in range(k * step, (k + 1) * step):
            for i in range(rounds):
                for low in range(0, COLUMNS, 128):
                    at = g * entries + i * COLUMNS + low
                    code = codes[i, g, :, low : low + 128].astype(jnp.int32).astype(jnp.float32)
                    result[:, at : at + 128] = code * terms[0] - terms[1]
        put(k).start()
    for k in range(steps):
        put(k).wait()


def solution(mesh):
    n_seq, n_vocab = mesh.shape["seq"], mesh.shape["vocab"]
    side = int(round(n_seq**0.5))

    def local(hidden, picks, counts, norm_gain, head_weight):
        slots = picks.shape[1]
        entries, width = head_weight.shape
        positions, features = hidden.shape[1:]
        total = n_seq * slots // 2
        rows = total // n_seq
        dma = lambda *shape: [pltpu.SemaphoreType.DMA(shape)] * 2
        hbm = pl.BlockSpec(memory_space=pltpu.HBM)
        codes, terms = pl.pallas_call(
            functools.partial(kernel, (n_seq, n_vocab, side, slots, total)),
            out_shape=(
                jax.ShapeDtypeStruct((entries // COLUMNS, n_seq, slots, COLUMNS), jnp.int16),
                jax.ShapeDtypeStruct((2, slots, 128), jnp.float32),
            ),
            in_specs=[hbm, hbm, pl.BlockSpec(memory_space=pltpu.SMEM), hbm, hbm],
            out_specs=(hbm, hbm),
            scratch_shapes=[
                pltpu.VMEM((features, positions), jnp.bfloat16),
                pltpu.VMEM((1, slots), jnp.int32),
                pltpu.VMEM((features,), jnp.float32),
                pltpu.VMEM((entries, width), jnp.bfloat16),
                pltpu.VMEM((width, entries), jnp.bfloat16),
                pltpu.VMEM((n_seq, 8, 128), jnp.int32),
                pltpu.VMEM((n_vocab, 8, 128), jnp.float32),
                pltpu.VMEM((2, 8, 128), jnp.float32),
                pltpu.VMEM((n_seq, rows, features), jnp.bfloat16),
                pltpu.VMEM((n_seq, rows, features), jnp.bfloat16),
                pltpu.VMEM((rows, features), jnp.bfloat16),
                pltpu.VMEM((n_vocab // 2, rows, features), jnp.bfloat16),
                pltpu.VMEM((side, 2, 2, side, HALF, width // 2), jnp.bfloat16),
                pltpu.VMEM((2 * side * HALF, entries), jnp.float32),
                pltpu.VMEM((total + slots, entries), jnp.int32),
                pltpu.VMEM((total, 128), jnp.float32),
                pltpu.VMEM((entries // COLUMNS, n_seq, slots, COLUMNS), jnp.int16),
                pltpu.VMEM((2, slots, 128), jnp.float32),
                pltpu.VMEM((n_seq, 8, 128), jnp.float32),
                pltpu.VMEM((n_vocab, 8, 128), jnp.float32),
                pltpu.SemaphoreType.DMA((4,)),
                pltpu.SemaphoreType.DMA,
                pltpu.SemaphoreType.DMA((entries // COLUMNS,)),
                *[pltpu.SemaphoreType.DMA((2,))] * 7,
                *dma(entries // COLUMNS),
                *dma(2, side),
                *dma(2, side, side),
                *dma(2, side, side),
            ],
            compiler_params=pltpu.CompilerParams(
                collective_id=0, has_side_effects=True, vmem_limit_bytes=VMEM_BYTES
            ),
            cost_estimate=pl.CostEstimate(
                flops=2 * total * entries * width, bytes_accessed=2 * entries * width, transcendentals=2 * total * entries
            ),
        )(jnp.swapaxes(hidden[0], 0, 1), picks, counts, norm_gain, head_weight)
        return pl.pallas_call(
            decode,
            out_shape=jax.ShapeDtypeStruct((slots, n_seq * entries), jnp.float32),
            in_specs=[hbm, hbm],
            out_specs=hbm,
            scratch_shapes=[
                pltpu.VMEM(codes.shape, codes.dtype),
                pltpu.VMEM(terms.shape, terms.dtype),
                pltpu.VMEM((slots, n_seq * entries), jnp.float32),
                pltpu.SemaphoreType.DMA((4,)),
                pltpu.SemaphoreType.DMA,
                pltpu.SemaphoreType.DMA((4,)),
            ],
            compiler_params=pltpu.CompilerParams(vmem_limit_bytes=VMEM_BYTES),
        )(codes, terms)
    in_specs = (
        P("seq", None, "vocab"),
        P("seq", None),
        P("seq"),
        P("vocab"),
        P(("vocab", "seq"), None),
    )
    return jax.shard_map(local, mesh=mesh, in_specs=in_specs, out_specs=P("seq", "vocab"), check_vma=False)
```

```python
import functools

import jax
import jax.numpy as jnp
from jax import lax
from jax.experimental import pallas as pl
from jax.experimental.pallas import tpu as pltpu
from jax.sharding import PartitionSpec as P

SOFT_CAP = 30.0
EPSILON = 1e-06
CODE = 32767.0
HALF = 16
COLUMNS = 256
VMEM_BYTES = 63 << 20
MESH = pl.DeviceIdType.MESH


def iota(shape, dim):
    return lax.broadcasted_iota(jnp.int32, shape, dim)


def kernel(
    dims,
    hidden_ref,
    picks_ref,
    counts_ref,
    gain_ref,
    head_ref,
    codes_ref,
    terms_ref,
    hidden,
    picks,
    gain,
    head,
    turned,
    cnt,
    gains,
    squares,
    place,
    placed,
    block_out,
    feats,
    rows_x,
    partial,
    level,
    expo,
    send,
    terms,
    sums_a,
    sums_b,
    in_sem,
    terms_sem,
    own_sem,
    cnt_sem,
    gain_sem,
    sqs_sem,
    plc_sem,
    fea_sem,
    sma_sem,
    smb_sem,
    out_s, out_r,
    one_s, one_r,
    two_s, two_r,
    fwd_s, fwd_r,
):
    n_seq, n_vocab, side, slots, total = dims
    rows = total // n_seq
    width = head_ref.shape[1]
    entries = head_ref.shape[0]
    features = hidden_ref.shape[0]
    block_rows = 2 * side * HALF
    half_width = width // 2
    n_z = n_vocab // 2
    s = lax.axis_index("seq")
    v = lax.axis_index("vocab")
    x, y = s // side, s % side
    z, core = v // 2, v % 2
    sibling = 2 * z + (1 - core)

    def seq_peer(p):
        return (s + p) % n_seq

    def vocab_peer(p):
        return (v + p) % n_vocab

    loads = [
        pltpu.make_async_copy(ref, to, in_sem.at[i])
        for i, (ref, to) in enumerate(
            [(hidden_ref, hidden), (picks_ref, picks), (gain_ref, gain), (head_ref, head)]
        )
    ]
    for load in loads:
        load.start()

    barrier = pltpu.get_barrier_semaphore()

    def greet_seq(p, c):
        pl.semaphore_signal(barrier, inc=1, device_id={"seq": seq_peer(p)}, device_id_type=MESH)
        return c

    def greet_vocab(p, c):
        pl.semaphore_signal(barrier, inc=1, device_id={"vocab": vocab_peer(p)}, device_id_type=MESH)
        return c

    lax.fori_loop(1, n_seq, greet_seq, 0)
    lax.fori_loop(1, n_vocab, greet_vocab, 0)
    pl.semaphore_wait(barrier, n_seq + n_vocab - 2)

    def hops(p, size):
        return min(p, size - p)

    seq_steps = sorted(
        ((a, b) for a in range(side) for b in range(side) if a or b),
        key=lambda step: hops(step[0], side) + hops(step[1], side),
    )

    def exchange(axis, peers, src, dst, many, sems):
        def copy(peer, src, dst):
            return pltpu.make_async_remote_copy(
                src_ref=src, dst_ref=dst, send_sem=sems.at[0], recv_sem=sems.at[1],
                device_id={axis: peer}, device_id_type=MESH,
            )

        def start():
            for peer in peers:
                copy(peer, src(peer), dst).start()

        def received():
            copy(peers[0], many, many).wait_recv()

        def sent():
            copy(peers[0], many, many).wait_send()

        return start, received, sent

    seq_peers = [(x + a) % side * side + (y + b) % side for a, b in seq_steps]
    vocab_peers = [vocab_peer(p) for p in sorted(range(1, n_vocab), key=lambda p: -hops(p, n_vocab))]

    cnt[pl.ds(s, 1)] = jnp.full((1, 8, 128), counts_ref[0], jnp.int32)
    cnt_start, cnt_received, cnt_sent = exchange(
        "seq", seq_peers, lambda peer: cnt.at[s], cnt.at[s], cnt.at[pl.ds(0, n_seq - 1)], cnt_sem
    )
    cnt_start()

    loads[0].wait()
    loads[1].wait()
    one_hot = (iota((hidden.shape[1], slots), 0) == picks[...]).astype(jnp.bfloat16)
    selected = jnp.dot(hidden[...], one_hot, preferred_element_type=jnp.float32).astype(jnp.bfloat16)

    turn = 256 if width % 256 == 0 else width // 3

    def turn_some(i, c):
        at = pl.ds(pl.multiple_of(i * turn, turn), turn)
        turned[at, :] = head[:, at].T
        return c

    loads[3].wait()
    thirds = [width // turn * i // 3 for i in range(4)]
    lax.fori_loop(thirds[0], thirds[1], turn_some, 0)

    cnt_received()
    group = iota((n_seq, 8, 128), 0)
    every = cnt[...]
    offset = jnp.sum(jnp.where(group < s, every, 0), axis=0)[0:1, 0:1]
    count = jnp.sum(jnp.where(group == s, every, 0), axis=0)[0:1, 0:1]

    slot = iota((total, slots), 1)
    placing = ((iota((total, slots), 0) == offset + slot) & (slot < count)).astype(jnp.bfloat16)

    compact = lax.dot_general(
        placing, selected, (((1,), (1,)), ((), ())), preferred_element_type=jnp.float32
    ).astype(jnp.bfloat16)
    place[...] = compact.reshape(n_seq, rows, features)
    plc_start, plc_received, plc_sent = exchange(
        "seq", seq_peers, lambda peer: place.at[peer], placed.at[s], placed.at[pl.ds(0, n_seq - 1)], plc_sem
    )
    plc_start()
    loads[2].wait()
    line = gain[...].reshape(1, features)
    line = jnp.concatenate([line, jnp.zeros((1, -features % 128), jnp.float32)], axis=1)
    lines = [line[:, c : c + 128] for c in range(0, line.shape[1], 128)]
    lines.append(jnp.zeros((8 - len(lines), 128), jnp.float32))
    gains[pl.ds(v, 1)] = jnp.concatenate(lines, axis=0)[None]
    gain_start, gain_received, gain_sent = exchange(
        "vocab", vocab_peers, lambda peer: gains.at[v], gains.at[v], gains.at[pl.ds(0, n_vocab - 1)], gain_sem
    )
    gain_start()

    lax.fori_loop(thirds[1], thirds[2], turn_some, 0)
    placed[pl.ds(s, 1)] = place[pl.ds(s, 1)]
    plc_received()
    block = jnp.sum(placed[...].astype(jnp.float32), axis=0).astype(jnp.bfloat16)

    part_of = z // (n_z // 2)
    kept = core == part_of
    mine = v - part_of * n_z

    def along(p, src, dst):
        return pltpu.make_async_remote_copy(
            src_ref=src, dst_ref=dst, send_sem=fea_sem.at[0], recv_sem=fea_sem.at[1],
            device_id={"vocab": 2 * ((z + p) % n_z) + part_of}, device_id_type=MESH,
        )

    block_out[...] = block
    for p in sorted(range(1, n_z), key=lambda p: -hops(p, n_z)):
        along(p, block_out, feats.at[mine]).start()

    @pl.when(kept)
    def _():
        feats[pl.ds(mine, 1)] = block[None]

    @pl.when(jnp.logical_not(kept))
    def _():
        along(0, block_out, feats.at[mine]).start()

    lax.fori_loop(thirds[2], thirds[3], turn_some, 0)

    @pl.when(kept)
    def _():
        many = feats.at[pl.ds(0, n_z - 1)]
        along(1, many, many).wait_recv()

    @pl.when(jnp.logical_not(kept))
    def _():
        along(1, feats, feats).wait_recv()

    raw = jnp.concatenate([feats[i] for i in range(n_z)], axis=1).astype(jnp.float32)

    row_eye = iota((rows, 128), 0) == iota((rows, 128), 1)
    square = jnp.sum(jnp.where(row_eye, jnp.sum(raw * raw, axis=1, keepdims=True), 0.0), axis=0, keepdims=True)
    squares[pl.ds(core, 1)] = jnp.broadcast_to(square, (8, 128))[None]
    tell_squares = pltpu.make_async_remote_copy(
        src_ref=squares.at[core], dst_ref=squares.at[core], send_sem=sqs_sem.at[0], recv_sem=sqs_sem.at[1],
        device_id={"vocab": sibling}, device_id_type=MESH,
    )
    tell_squares.start()
    gain_received()
    held = gains[pl.ds(core * n_z, n_z)]
    scale = jnp.concatenate(
        [held[i, c // 128 : c // 128 + 1, : min(128, features - c)] for i in range(n_z) for c in range(0, features, 128)],
        axis=1,
    )
    tell_squares.wait_recv()
    mean_square = jnp.sum(squares[...], axis=0)[0:1] / width
    mean_square = jnp.sum(jnp.where(row_eye, mean_square, 0.0), axis=1, keepdims=True)
    own = (raw * lax.rsqrt(mean_square + EPSILON) * scale).astype(jnp.bfloat16)
    rows_x[0, pl.ds(core, 1), 0, 0] = own[:HALF][None]
    rows_x[0, pl.ds(core, 1), 1, 0] = own[HALF:][None]

    def across(order, p):
        if order == 0:
            return ((x + p) % side) * side + y
        return x * side + (y + p) % side

    def hop(src, dst, sems, j, order, p):
        return pltpu.make_async_remote_copy(
            src_ref=src, dst_ref=dst, send_sem=sems[0].at[j], recv_sem=sems[1].at[j],
            device_id={"seq": across(order, p)}, device_id_type=MESH,
        )

    def first(order, j):
        return hop(rows_x.at[0, core, order, 0], rows_x.at[j, core, order, 0], (one_s, one_r), j, order, j)

    def first_both(j):
        many = rows_x.at[j, core, :, 0]
        return hop(many, many, (one_s, one_r), j, 0, j)

    def second(order, j, p):
        return hop(rows_x.at[j, core, order, 0], rows_x.at[j, core, order, p], (two_s, two_r), j, 1 - order, p)

    def second_all(j):
        many = rows_x.at[j, core, :, pl.ds(1, side - 1)]
        return hop(many, many, (two_s, two_r), j, 0, 1)

    def over(kind, j):
        at = rows_x.at[j, kind]
        return pltpu.make_async_remote_copy(
            src_ref=at, dst_ref=at, send_sem=fwd_s.at[j], recv_sem=fwd_r.at[j],
            device_id={"vocab": sibling}, device_id_type=MESH,
        )

    near = [p for d in range(1, side // 2 + 1) for p in sorted({d, side - d})]
    for j in near:
        for order in range(2):
            first(order, j).start()
    for p in near:
        for order in range(2):
            second(order, 0, p).start()
    def spread(j):
        first_both(j).wait_recv()
        for p in near:
            for order in range(2):
                second(order, j, p).start()

    for j in near[:-1]:
        spread(j)

    level[pl.ds(total, slots)] = jnp.zeros((slots, entries), jnp.int32)
    rounds = entries // COLUMNS

    def row_of(order, j, p):
        if order == 0:
            return ((x + side - j) % side * side + (y + side - p) % side) * rows
        return ((x + side - p) % side * side + (y + side - j) % side) * rows + HALF

    def product(j, k, i):
        at = pl.ds(pl.multiple_of(i * COLUMNS, COLUMNS), COLUMNS)
        return at, lax.dot_general(
            rows_x[j, k].reshape(block_rows, half_width),
            turned[pl.ds(pl.multiple_of(k * half_width, half_width), half_width), at],
            (((1,), (0,)), ((), ())),
            preferred_element_type=jnp.float32,
        )

    def fill(i):
        at = i * COLUMNS

        def one(g, c):
            start = jnp.sum(jnp.where(group < g, cnt[...], 0), axis=0)[0:1, 0:1]
            for low in range(0, COLUMNS, 128):
                window = level[:, pl.ds(pl.multiple_of(at + low, 128), 128)]
                bit = 1 << (total.bit_length() - 2)
                while bit:
                    left = bit - 1 + slots if bit > 8 else slots + 8
                    left = (left + 7) // 8 * 8
                    if bit >= 8:
                        window = jnp.where(start & bit != 0, window[bit : bit + left], window[:left])
                    else:
                        window = jnp.where(start & bit != 0, pltpu.roll(window, left - bit, axis=0), window)
                    bit //= 2
                send[pl.ds(i, 1), pl.ds(g, 1), :, low : low + 128] = window[:slots].astype(jnp.int16)[None, None]
            return c

        lax.fori_loop(0, n_seq, one, 0)
        keep(i).start()

    def keep(i):
        return pltpu.make_async_copy(send.at[i, s], codes_ref.at[i, s], own_sem.at[i])

    def returned(i, peer, src, dst):
        return pltpu.make_async_remote_copy(
            src_ref=src, dst_ref=dst, send_sem=out_s.at[i], recv_sem=out_r.at[i],
            device_id={"seq": peer}, device_id_type=MESH,
        )

    def give(i):
        for peer in seq_peers:
            returned(i, peer, send.at[i, peer], codes_ref.at[i, s]).start()

    def all_returned(i):
        many = codes_ref.at[i, pl.ds(0, n_seq - 1)]
        return returned(i, seq_peers[0], many, many)

    last = near[-1]

    def begin_block(j):
        def some(i, c):
            at, logits = product(j, core, i)
            partial[:, at] = logits
            return c

        lax.fori_loop(0, rounds, some, 0)

    def end_block(j):
        def some(i, total_exp):
            at, logits = product(j, 1 - core, i)
            bent = jnp.tanh((logits + partial[:, at]) / SOFT_CAP)
            code = jnp.round(bent * CODE).astype(jnp.int32)
            for order in range(2):
                for p in range(side):
                    low = (order * side + p) * HALF
                    level[pl.ds(pl.multiple_of(row_of(order, j, p), HALF), HALF), at] = code[low : low + HALF]
            e = jnp.exp(SOFT_CAP * bent)
            for c in range(0, COLUMNS, 128):
                total_exp += e[:, c : c + 128]
            if j == last:
                fill(i)

                @pl.when(i == 0)
                def _():
                    give(0)

            return total_exp

        total_exp = lax.fori_loop(0, rounds, some, jnp.zeros((block_rows, 128), jnp.float32))
        summed = jnp.broadcast_to(jnp.sum(total_exp, axis=1, keepdims=True), total_exp.shape)
        for order in range(2):
            for p in range(side):
                low = (order * side + p) * HALF
                expo[pl.ds(pl.multiple_of(row_of(order, j, p), HALF), HALF)] = summed[low : low + HALF]

    for j in [0] + near:
        second_all(j).wait_recv()
        over(core, j).start()
        if j == 0:
            spread(last)
        begin_block(j)
        over(1 - core, j).wait_recv()
        end_block(j)

    square_eye = iota((128, 128), 0) == iota((128, 128), 1)
    lines = [
        jnp.sum(jnp.where(square_eye, expo[i * 128 : (i + 1) * 128], 0.0), axis=0, keepdims=True)
        for i in range(total // 128)
    ]
    lines.append(jnp.zeros((8 - len(lines), 128), jnp.float32))
    sums_a[pl.ds(s, 1)] = jnp.concatenate(lines, axis=0)[None]
    sma_start, sma_received, sma_sent = exchange(
        "seq", seq_peers, lambda peer: sums_a.at[s], sums_a.at[s], sums_a.at[pl.ds(0, n_seq - 1)], sma_sem
    )
    sma_start()

    for i in range(1, rounds):
        give(i)

    sma_received()
    sums_b[pl.ds(v, 1)] = jnp.sum(sums_a[...], axis=0)[None]
    smb_start, smb_received, smb_sent = exchange(
        "vocab", vocab_peers, lambda peer: sums_b.at[v], sums_b.at[v], sums_b.at[pl.ds(0, n_vocab - 1)], smb_sem
    )
    smb_start()
    smb_received()
    partition = jnp.sum(sums_b[...], axis=0)
    total_of = jnp.zeros((slots, 1), jnp.float32)
    for i in range(total // 128):
        hit = iota((slots, 128), 1) + 128 * i == offset + iota((slots, 128), 0)
        total_of += jnp.sum(jnp.where(hit, partition[i : i + 1], 0.0), axis=1, keepdims=True)
    live = iota((slots, 128), 0) < count
    terms[0] = jnp.where(live, SOFT_CAP / CODE, 0.0)
    terms[1] = jnp.where(live, jnp.log(jnp.where(total_of > 0.0, total_of, 1.0)), 0.0)
    write_terms = pltpu.make_async_copy(terms, terms_ref, terms_sem)
    write_terms.start()

    cnt_sent()
    gain_sent()
    plc_sent()
    tell_squares.wait_send()

    @pl.when(kept)
    def _():
        many = feats.at[pl.ds(0, n_z - 1)]
        along(1, many, many).wait_send()

    @pl.when(jnp.logical_not(kept))
    def _():
        along(1, feats, feats).wait_send()

    for j in near:
        first_both(j).wait_send()
    for j in [0] + near:
        second_all(j).wait_send()
        over(core, j).wait_send()
    sma_sent()
    smb_sent()
    write_terms.wait()
    for i in range(rounds):
        keep(i).wait()
        all_returned(i).wait()


def decode(codes_ref, terms_ref, out_ref, codes, terms, result, codes_sem, terms_sem, out_sem):
    rounds, n_seq, slots, _ = codes_ref.shape
    entries = rounds * COLUMNS
    steps = 4
    step = n_seq // steps
    take_terms = pltpu.make_async_copy(terms_ref, terms, terms_sem)
    take_terms.start()

    def take(k):
        at = pl.ds(k * step, step)
        return pltpu.make_async_copy(codes_ref.at[:, at], codes.at[:, at], codes_sem.at[k])

    def put(k):
        at = pl.ds(k * step * entries, step * entries)
        return pltpu.make_async_copy(result.at[:, at], out_ref.at[:, at], out_sem.at[k])

    for k in range(steps):
        take(k).start()
    take_terms.wait()
    for k in range(steps):
        take(k).wait()
        for g in range(k * step, (k + 1) * step):
            for i in range(rounds):
                for low in range(0, COLUMNS, 128):
                    at = g * entries + i * COLUMNS + low
                    code = codes[i, g, :, low : low + 128].astype(jnp.int32).astype(jnp.float32)
                    result[:, at : at + 128] = code * terms[0] - terms[1]
        put(k).start()
    for k in range(steps):
        put(k).wait()


def solution(mesh):
    n_seq, n_vocab = mesh.shape["seq"], mesh.shape["vocab"]
    side = int(round(n_seq**0.5))

    def local(hidden, picks, counts, norm_gain, head_weight):
        slots = picks.shape[1]
        entries, width = head_weight.shape
        positions, features = hidden.shape[1:]
        total = n_seq * slots // 2
        rows = total // n_seq
        dma = lambda *shape: [pltpu.SemaphoreType.DMA(shape)] * 2
        hbm = pl.BlockSpec(memory_space=pltpu.HBM)
        codes, terms = pl.pallas_call(
            functools.partial(kernel, (n_seq, n_vocab, side, slots, total)),
            out_shape=(
                jax.ShapeDtypeStruct((entries // COLUMNS, n_seq, slots, COLUMNS), jnp.int16),
                jax.ShapeDtypeStruct((2, slots, 128), jnp.float32),
            ),
            in_specs=[hbm, hbm, pl.BlockSpec(memory_space=pltpu.SMEM), hbm, hbm],
            out_specs=(hbm, hbm),
            scratch_shapes=[
                pltpu.VMEM((features, positions), jnp.bfloat16),
                pltpu.VMEM((1, slots), jnp.int32),
                pltpu.VMEM((features,), jnp.float32),
                pltpu.VMEM((entries, width), jnp.bfloat16),
                pltpu.VMEM((width, entries), jnp.bfloat16),
                pltpu.VMEM((n_seq, 8, 128), jnp.int32),
                pltpu.VMEM((n_vocab, 8, 128), jnp.float32),
                pltpu.VMEM((2, 8, 128), jnp.float32),
                pltpu.VMEM((n_seq, rows, features), jnp.bfloat16),
                pltpu.VMEM((n_seq, rows, features), jnp.bfloat16),
                pltpu.VMEM((rows, features), jnp.bfloat16),
                pltpu.VMEM((n_vocab // 2, rows, features), jnp.bfloat16),
                pltpu.VMEM((side, 2, 2, side, HALF, width // 2), jnp.bfloat16),
                pltpu.VMEM((2 * side * HALF, entries), jnp.float32),
                pltpu.VMEM((total + slots, entries), jnp.int32),
                pltpu.VMEM((total, 128), jnp.float32),
                pltpu.VMEM((entries // COLUMNS, n_seq, slots, COLUMNS), jnp.int16),
                pltpu.VMEM((2, slots, 128), jnp.float32),
                pltpu.VMEM((n_seq, 8, 128), jnp.float32),
                pltpu.VMEM((n_vocab, 8, 128), jnp.float32),
                pltpu.SemaphoreType.DMA((4,)),
                pltpu.SemaphoreType.DMA,
                pltpu.SemaphoreType.DMA((entries // COLUMNS,)),
                *[pltpu.SemaphoreType.DMA((2,))] * 7,
                *dma(entries // COLUMNS),
                *dma(side),
                *dma(side),
                *dma(side),
            ],
            compiler_params=pltpu.CompilerParams(
                collective_id=0, has_side_effects=True, vmem_limit_bytes=VMEM_BYTES
            ),
            cost_estimate=pl.CostEstimate(
                flops=2 * total * entries * width, bytes_accessed=2 * entries * width, transcendentals=2 * total * entries
            ),
        )(jnp.swapaxes(hidden[0], 0, 1), picks, counts, norm_gain, head_weight)
        return pl.pallas_call(
            decode,
            out_shape=jax.ShapeDtypeStruct((slots, n_seq * entries), jnp.float32),
            in_specs=[hbm, hbm],
            out_specs=hbm,
            scratch_shapes=[
                pltpu.VMEM(codes.shape, codes.dtype),
                pltpu.VMEM(terms.shape, terms.dtype),
                pltpu.VMEM((slots, n_seq * entries), jnp.float32),
                pltpu.SemaphoreType.DMA((4,)),
                pltpu.SemaphoreType.DMA,
                pltpu.SemaphoreType.DMA((4,)),
            ],
            compiler_params=pltpu.CompilerParams(vmem_limit_bytes=VMEM_BYTES),
        )(codes, terms)
    in_specs = (
        P("seq", None, "vocab"),
        P("seq", None),
        P("seq"),
        P("vocab"),
        P(("vocab", "seq"), None),
    )
    return jax.shard_map(local, mesh=mesh, in_specs=in_specs, out_specs=P("seq", "vocab"), check_vma=False)
```
